128 devices in a mesh: row: 8 (over z, y_lo), col: 16 (over y_hi, x, core).
Axes of the slice: x: 4, y: 4 (y_hi: 2, y_lo: 2; y = y_hi * 2 + y_lo), z: 4, core: 2. Of those that a mesh axis runs over, the one named last changes fastest.
Arguments:
- subspace: bfloat16 [1024, 12288], P('col', 'row')
- rotation: bfloat16 [1024, 1024], replicated, may hold values from -0.1875 to 0.1875
- block_tiles: bfloat16 [64, 31, 192, 192], P('row'), as said below
- block_cols: int32 [64, 31], P('row'), may hold values from 0 to 63, as said below
Outputs:
- filtered: bfloat16 [1024, 12288], P('col', 'row')
- gram_matrix: float32 [1024, 1024], P('col', 'row')
- rayleigh: float32 [1024, 1024], P('col', 'row')
The draws below stay inside these ranges and needn't reach their ends.
Inputs may be any that keep to these rules, and one draw needn't show every extreme that they name: block_cols[i, 0] = i; for t < 15, block_cols[i, 2t+1] = p_t(i) and block_cols[i, 2t+2] is the inverse of p_t at i, where each p_t is a permutation of the 64 block rows. The stored matrix is symmetric: block_tiles[i, 0] is symmetric and block_tiles[i, 2t+2] is the transpose of block_tiles[j, 2t+1] for the block row j with block_cols[j, 2t+1] = i.
All inputs are finite; a program needn't handle non-finite values.
Results may differ from the reference program's by a relative error of at most 0.014.
Values may be sent and summed in bfloat16 or wider, within the bound.
A program may use at most 128 MiB of HBM per device.

```python
import math
import jax
import jax.numpy as jnp
from jax import lax

M = 1024
BLK = 192
DEGREE = 4
PAIRS = 15
NBLK = 64
NROWS = 12288


def pattern_permutes(key):
    permutes = jnp.stack([jax.random.permutation(jax.random.fold_in(key, 500 + pair_index), NBLK) for pair_index in range(PAIRS)]).astype(jnp.int32)
    inverse = jnp.argsort(permutes, axis=1).astype(jnp.int32)
    return (permutes, inverse)


def draw_block_cols(key, part):
    permutes, inverse = pattern_permutes(key)
    identity = jnp.arange(NBLK, dtype=jnp.int32)
    columns = [identity]
    for pair_index in range(PAIRS):
        columns.append(permutes[pair_index])
        columns.append(inverse[pair_index])
    return jnp.stack(columns, axis=1).astype(jnp.int32)


def draw_block_tiles(key, part):
    permutes, inverse = pattern_permutes(key)
    key = jax.random.fold_in(key, 31)
    first_key, second_key, third_key = jax.random.split(key, 3)
    off_scale = 0.35 / math.sqrt(2 * PAIRS * BLK)
    pair_tiles = jax.random.normal(first_key, (PAIRS, NBLK, BLK, BLK), jnp.float32) * off_scale
    diag_noise = jax.random.normal(second_key, (NBLK, BLK, BLK), jnp.float32) * (0.4 / (2.0 * math.sqrt(2 * BLK)))
    diag_level = jax.random.uniform(third_key, (NBLK,), jnp.float32, 1.0, 1.5)
    diagonal = diag_level[:, None, None] * jnp.eye(BLK, dtype=jnp.float32) + diag_noise + jnp.swapaxes(diag_noise, 1, 2)
    stored = [diagonal]
    for pair_index in range(PAIRS):
        stored.append(pair_tiles[pair_index])
        stored.append(jnp.swapaxes(pair_tiles[pair_index][inverse[pair_index]], 1, 2))
    return jnp.stack(stored, axis=1).astype(jnp.bfloat16)


def draw_subspace(key, part):
    key = jax.random.fold_in(key, 11)
    first_key, second_key = jax.random.split(key, 2)
    position = jnp.arange(NROWS, dtype=jnp.float32) / NROWS
    rough_part = jax.random.uniform(second_key, (NROWS,), jnp.float32, 0.0, 1.0)
    row_scale = jnp.power(3.0, position) * jnp.power(10.0, rough_part) / 8.0
    values = jax.random.normal(first_key, (M, NROWS), jnp.float32)
    return (values * row_scale[None, :]).astype(jnp.bfloat16)


def scatter_about(own_key, extent, scale, limit, held_as=jnp.bfloat16):
    result = jax.random.normal(own_key, extent, jnp.float32) * scale
    return jnp.minimum(jnp.maximum(result, -limit), limit).astype(held_as)


def setup_inputs(seed: int = 0) -> dict:
    seeds = jax.random.split(jax.random.key(seed), 5)
    subspace = draw_subspace(jax.random.fold_in(seeds[4], 71), 0)
    rotation = scatter_about(seeds[1], (M, M), M ** -0.5, 0.1875)
    block_tiles = draw_block_tiles(jax.random.fold_in(seeds[4], 71), 0)
    block_cols = draw_block_cols(jax.random.fold_in(seeds[4], 71), 0)
    return dict(subspace=subspace, rotation=rotation, block_tiles=block_tiles, block_cols=block_cols)


filter_center = 1.6
filter_width = 0.9


def apply_matrix(vectors, block_tiles, block_cols):
    by_block = vectors.reshape(M, NBLK, BLK).astype(jnp.float32)
    slot_tiles = jnp.moveaxis(block_tiles, 1, 0)
    slot_cols = jnp.transpose(block_cols).astype(jnp.int32)

    def add_slot(running, slot_pair):
        columns, tiles_now = slot_pair
        picked = jnp.take(by_block, columns, axis=1)
        return running + jnp.einsum('mib,iab->mia', picked, tiles_now.astype(jnp.float32)), None

    running, _ = lax.scan(add_slot, jnp.zeros((M, NBLK, BLK), jnp.float32), (slot_cols, slot_tiles))
    return running.reshape(M, NROWS)


def reference(subspace, rotation, block_tiles, block_cols):
    rotated = jnp.dot(jnp.transpose(rotation), subspace, preferred_element_type=jnp.float32).astype(jnp.bfloat16)
    previous = rotated
    applied = apply_matrix(previous, block_tiles, block_cols)
    current = ((applied - filter_center * previous.astype(jnp.float32)) / filter_width).astype(jnp.bfloat16)
    for level_index in range(DEGREE - 1):
        applied = apply_matrix(current, block_tiles, block_cols)
        following = (2.0 / filter_width) * (applied - filter_center * current.astype(jnp.float32)) - previous.astype(jnp.float32)
        previous = current
        current = following.astype(jnp.bfloat16)
    filtered = current
    images = apply_matrix(filtered, block_tiles, block_cols).astype(jnp.bfloat16)
    inverse_rows = 1.0 / NROWS
    gram_matrix = jnp.dot(filtered, jnp.transpose(filtered), preferred_element_type=jnp.float32) * inverse_rows
    rayleigh = jnp.dot(filtered, jnp.transpose(images), preferred_element_type=jnp.float32) * inverse_rows
    return filtered, gram_matrix, rayleigh
```

```python
import functools

import jax
import jax.numpy as jnp
from jax import lax
from jax.experimental import pallas as pl
from jax.experimental.pallas import tpu as pltpu
from jax.sharding import PartitionSpec as P

MESH = pl.DeviceIdType.MESH
DEGREE = 4
CENTER = 1.6
WIDTH = 0.9
ROWS = 8
COLS = 16
BLK = 192
SLOTS = 31
PAIRS = 4
HALF = PAIRS * BLK
PIECE = HALF // COLS
LANES = 128


def swap_halves(values):
    return pltpu.roll(values, LANES // 2, 1)


def kernel(
    cols, sub, rot_hbm, tiles_hbm, filt, gram, ray,
    field0, field1, tiles, rot, packed, raw, mixed, peer, merged, every, terms, parts,
    load_sem, rot_sem, out1, in1, out2, in2, row_out, row_in,
    sib_out, sib_in, col_out, col_in, sum_out, sum_in,
):
    r = lax.axis_index("row")
    c = lax.axis_index("col")
    core = lax.rem(c, 2)
    chip = c // 2
    sibling = c + 1 - 2 * core
    f32, bf16 = jnp.float32, jnp.bfloat16
    fields = (field0, field1)
    lane = lax.broadcasted_iota(jnp.int32, (1, LANES), 1) // (LANES // 2)

    loads = [pltpu.make_async_copy(tiles_hbm.at[i], tiles.at[i], load_sem.at[i]) for i in range(8)]
    rot_load = pltpu.make_async_copy(rot_hbm, rot, rot_sem)
    rot_load.start()
    for load in loads:
        load.start()

    def send(src, dst, out_sem, in_sem, to_row, to_col):
        copy = pltpu.make_async_remote_copy(
            src_ref=src, dst_ref=dst, send_sem=out_sem, recv_sem=in_sem,
            device_id=(to_row, to_col), device_id_type=MESH,
        )
        return copy

    barrier = pltpu.get_barrier_semaphore()
    for d in range(1, COLS):
        pl.semaphore_signal(barrier, inc=1, device_id=(r, lax.rem(c + d, COLS)), device_id_type=MESH)
    for d in range(1, ROWS):
        for k in (0, 1):
            pl.semaphore_signal(
                barrier, inc=1, device_id=(lax.rem(r + d, ROWS), 2 * chip + k), device_id_type=MESH
            )

    natural = jnp.concatenate([sub[:, :HALF], sub[:, HALF:]], axis=0).astype(f32)
    packed[...] = natural.T.astype(bf16)
    for q in range(PAIRS):
        field1[PAIRS * r + q] = jnp.zeros((BLK, LANES), bf16)
    pl.semaphore_wait(barrier, COLS - 1 + 2 * (ROWS - 1))

    sends = []
    for d in range(1, COLS):
        to = lax.rem(c + d, COLS)
        copy = send(
            packed.at[pl.ds(pl.multiple_of(to * PIECE, PIECE), PIECE)], raw.at[c],
            out1.at[d], in1.at[c], r, to,
        )
        copy.start()
        sends.append(copy)
    raw[c] = packed[pl.ds(pl.multiple_of(c * PIECE, PIECE), PIECE), :]
    for d in range(1, COLS):
        src = lax.rem(c + d, COLS)
        send(packed.at[pl.ds(0, PIECE)], raw.at[src], out1.at[d], in1.at[src], r, src).wait_recv()
    rot_load.wait()
    left, right = [], []
    for e in range(COLS // 2):
        a, b = raw[2 * e].astype(f32), raw[2 * e + 1].astype(f32)
        left.append(jnp.where(lane == 0, a, swap_halves(b)))
        right.append(jnp.where(lane == 0, swap_halves(a), b))
    wide = jnp.concatenate(
        [jnp.concatenate(left, axis=1), jnp.concatenate(right, axis=1)], axis=0
    ).astype(bf16)
    rotated = jnp.dot(wide, rot[...], preferred_element_type=f32)
    for e in range(COLS // 2):
        a = rotated[:PIECE, e * LANES : (e + 1) * LANES]
        b = rotated[PIECE:, e * LANES : (e + 1) * LANES]
        mixed[2 * e] = jnp.where(lane == 0, a, swap_halves(b)).astype(bf16)
        mixed[2 * e + 1] = jnp.where(lane == 0, swap_halves(a), b).astype(bf16)

    def piece(of):
        return PAIRS * r + of // PAIRS, pl.ds(pl.multiple_of(lax.rem(of, PAIRS) * PIECE, PIECE), PIECE)

    for d in range(1, COLS):
        to = lax.rem(c + d, COLS)
        copy = send(mixed.at[to], field0.at[*piece(c)], out2.at[d], in2.at[c], r, to)
        copy.start()
        sends.append(copy)
    field0[*piece(c)] = mixed[c]
    for d in range(1, COLS):
        src = lax.rem(c + d, COLS)
        send(mixed.at[0], field0.at[*piece(src)], out2.at[d], in2.at[src], r, src).wait_recv()
    for copy in sends:
        copy.wait_send()

    def chunk_rows(q):
        return pl.ds(pl.multiple_of(q * BLK, BLK), BLK)

    def row_copy(par, q, d, src_row, to_row):
        view = fields[par].at[PAIRS * src_row + q]
        return send(view, view, row_out.at[q, d], row_in.at[par, q, src_row], to_row, c)

    def spread(par, q):
        for d in range(1, ROWS):
            row_copy(par, q, d, r, lax.rem(r + d, ROWS)).start()

    def await_all(par):
        def step(q, carry):
            for d in range(1, ROWS):
                row_copy(par, q, d, lax.rem(r + d, ROWS), r).wait_recv()
                row_copy(par, q, d, r, r).wait_send()
            return carry

        lax.fori_loop(0, PAIRS, step, 0)

    def block_row(par, i):
        total = jnp.zeros((BLK, LANES), f32)
        for s in range(SLOTS):
            col = cols[i, s]
            part = fields[par][((col >> 3) << 2) + (col & 3)]
            part = jnp.where(lane == ((col >> 2) & 1), part, jnp.zeros_like(part))
            total += jnp.dot(tiles[i, s], part, preferred_element_type=f32)
        return total + swap_halves(total)

    def applied(par, q):
        return jnp.where(lane == 0, block_row(par, q), block_row(par, q + PAIRS))

    def next_level(par, q, scale):
        now = fields[par][PAIRS * r + q].astype(f32)
        before = fields[1 - par][PAIRS * r + q].astype(f32)
        level = scale * (applied(par, q) - CENTER * now) - before
        fields[1 - par][PAIRS * r + q] = level.astype(bf16)

    lax.fori_loop(0, PAIRS, lambda q, x: (spread(0, q), x)[1], 0)
    for load in loads:
        load.wait()

    def one_level(par, scale):
        await_all(par)

        def pair(q, carry):
            next_level(par, q, scale)
            spread(1 - par, q)
            return carry

        lax.fori_loop(0, PAIRS, pair, 0)

    def two_levels(k, carry):
        one_level(0, jnp.where(k == 0, 1.0 / WIDTH, 2.0 / WIDTH))
        one_level(1, 2.0 / WIDTH)
        return carry

    lax.fori_loop(0, DEGREE // 2, two_levels, 0)

    def sib_copy(which, q):
        src = fields[which].at[PAIRS * r + q]
        return send(
            src, peer.at[which, chunk_rows(q)], sib_out.at[which, q], sib_in.at[which, q], r, sibling
        )

    def whole(which):
        return jnp.concatenate([fields[which][PAIRS * r + q] for q in range(PAIRS)], axis=0).astype(f32)

    def merge(which):
        own = whole(which)
        other = swap_halves(peer[which].astype(f32))
        return jnp.where(lane == core, own, other)

    for q in range(PAIRS):
        sib_copy(0, q).start()
    flat = whole(0).T.astype(bf16)
    filt[:, :HALF] = flat[: LANES // 2]
    filt[:, HALF:] = flat[LANES // 2 :]
    for q in range(PAIRS):
        sib_copy(0, q).wait()
    own_half = merge(0)
    every[chip] = own_half.astype(bf16)
    merged[:LANES, :] = own_half.T.astype(bf16)

    def col_copy(d, src_chip, to_chip):
        return send(
            every.at[src_chip], every.at[src_chip], col_out.at[d], col_in.at[src_chip],
            r, 2 * to_chip + core,
        )

    for d in range(1, ROWS):
        col_copy(d, chip, lax.rem(chip + d, ROWS)).start()

    await_all(0)

    def image_pair(q, carry):
        field1[PAIRS * r + q] = applied(0, q).astype(bf16)
        sib_copy(1, q).start()
        return carry

    lax.fori_loop(0, PAIRS, image_pair, 0)
    for q in range(PAIRS):
        sib_copy(1, q).wait()
    merged[LANES:, :] = merge(1).T.astype(bf16)
    for d in range(1, ROWS):
        col_copy(d, lax.rem(chip + d, ROWS), chip).wait_recv()
        col_copy(d, chip, chip).wait_send()

    for e in range(ROWS):
        product = jnp.dot(merged[...], every[e], preferred_element_type=f32).astype(bf16)
        for k in range(2):
            low = k * LANES // 2
            terms[e, k, : LANES // 2] = product[low : low + LANES // 2]
            terms[e, k, LANES // 2 :] = product[LANES + low : LANES + low + LANES // 2]

    source = 2 * r + core

    def sum_copy(n, to_row, to_core, src):
        return send(
            terms.at[to_row, to_core], parts.at[src], sum_out.at[n], sum_in.at[src],
            to_row, 2 * chip + to_core,
        )

    def member(n):
        index = lax.rem(source + n, 2 * ROWS)
        return index // 2, lax.rem(index, 2), index

    for n in range(1, 2 * ROWS):
        to_row, to_core, _ = member(n)
        sum_copy(n, to_row, to_core, source).start()
    parts[source] = terms[r, core]
    for n in range(1, 2 * ROWS):
        _, _, index = member(n)
        sum_copy(n, r, core, index).wait_recv()
        sum_copy(n, r, core, index).wait_send()
    total = parts[0].astype(f32)
    for n in range(1, 2 * ROWS):
        total += parts[n].astype(f32)
    total *= 1.0 / (ROWS * 2 * HALF)
    gram[...] = total[: LANES // 2]
    ray[...] = total[LANES // 2 :]


def local(subspace, rotation, block_tiles, block_cols):
    bf16, f32 = jnp.bfloat16, jnp.float32
    vmem = pl.BlockSpec(memory_space=pltpu.VMEM)
    dma = pltpu.SemaphoreType.DMA
    return pl.pallas_call(
        kernel,
        out_shape=(
            jax.ShapeDtypeStruct(subspace.shape, bf16),
            jax.ShapeDtypeStruct((LANES // 2, LANES), f32),
            jax.ShapeDtypeStruct((LANES // 2, LANES), f32),
        ),
        in_specs=[
            pl.BlockSpec(memory_space=pltpu.SMEM),
            vmem,
            pl.BlockSpec(memory_space=pl.ANY),
            pl.BlockSpec(memory_space=pl.ANY),
        ],
        out_specs=(vmem, vmem, vmem),
        scratch_shapes=[
            pltpu.VMEM((ROWS * PAIRS, BLK, LANES), bf16),
            pltpu.VMEM((ROWS * PAIRS, BLK, LANES), bf16),
            pltpu.VMEM(block_tiles.shape, bf16),
            pltpu.VMEM(rotation.shape, bf16),
            pltpu.VMEM((HALF, LANES), bf16),
            pltpu.VMEM((COLS, PIECE, LANES), bf16),
            pltpu.VMEM((COLS, PIECE, LANES), bf16),
            pltpu.VMEM((2, HALF, LANES), bf16),
            pltpu.VMEM((2 * LANES, HALF), bf16),
            pltpu.VMEM((ROWS, HALF, LANES), bf16),
            pltpu.VMEM((ROWS, 2, LANES, LANES), bf16),
            pltpu.VMEM((2 * ROWS, LANES, LANES), bf16),
            dma((8,)),
            dma,
            dma((COLS,)),
            dma((COLS,)),
            dma((COLS,)),
            dma((COLS,)),
            dma((PAIRS, ROWS)),
            dma((2, PAIRS, ROWS)),
            dma((2, PAIRS)),
            dma((2, PAIRS)),
            dma((ROWS,)),
            dma((ROWS,)),
            dma((2 * ROWS,)),
            dma((2 * ROWS,)),
        ],
        compiler_params=pltpu.CompilerParams(
            collective_id=0, has_side_effects=True, vmem_limit_bytes=56 * 2**20
        ),
        cost_estimate=pl.CostEstimate(flops=7_000_000_000, bytes_accessed=30_000_000, transcendentals=0),
    )(block_cols, subspace, rotation, block_tiles)


def solution(mesh):
    return jax.shard_map(
        local,
        mesh=mesh,
        in_specs=(P("col", "row"), P(), P("row", None, None, None), P("row", None)),
        out_specs=(P("col", "row"), P("col", "row"), P("col", "row")),
        check_vma=False,
    )
```

```python
import functools

import jax
import jax.numpy as jnp
from jax import lax
from jax.experimental import pallas as pl
from jax.experimental.pallas import tpu as pltpu
from jax.sharding import PartitionSpec as P

MESH = pl.DeviceIdType.MESH
DEGREE = 4
CENTER = 1.6
WIDTH = 0.9
ROWS = 8
COLS = 16
BLK = 192
SLOTS = 31
PAIRS = 4
HALF = PAIRS * BLK
PIECE = HALF // COLS
LAG = 2
LANES = 128


def swap_halves(values):
    return pltpu.roll(values, LANES // 2, 1)


def kernel(
    cols, sub, rot_hbm, tiles_hbm, filt, gram, ray,
    field0, field1, tiles, rot, packed, raw, mixed, peer, every, terms, parts,
    load_sem, rot_sem, out1, in1, out2, in2, row_out, row_in,
    sib_out, sib_in, col_out, col_in, sum_out, sum_in,
):
    r = lax.axis_index("row")
    c = lax.axis_index("col")
    core = lax.rem(c, 2)
    chip = c // 2
    sibling = c + 1 - 2 * core
    f32, bf16 = jnp.float32, jnp.bfloat16
    fields = (field0, field1)
    lane = lax.broadcasted_iota(jnp.int32, (1, LANES), 1) // (LANES // 2)

    loads = [pltpu.make_async_copy(tiles_hbm.at[i], tiles.at[i], load_sem.at[i]) for i in range(8)]
    rot_load = pltpu.make_async_copy(rot_hbm, rot, rot_sem)
    rot_load.start()
    for load in loads:
        load.start()

    def send(src, dst, out_sem, in_sem, to_row, to_col):
        copy = pltpu.make_async_remote_copy(
            src_ref=src, dst_ref=dst, send_sem=out_sem, recv_sem=in_sem,
            device_id=(to_row, to_col), device_id_type=MESH,
        )
        return copy

    barrier = pltpu.get_barrier_semaphore()
    for d in range(1, COLS):
        pl.semaphore_signal(barrier, inc=1, device_id=(r, lax.rem(c + d, COLS)), device_id_type=MESH)
    for d in range(1, ROWS):
        for k in (0, 1):
            pl.semaphore_signal(
                barrier, inc=1, device_id=(lax.rem(r + d, ROWS), 2 * chip + k), device_id_type=MESH
            )

    natural = jnp.concatenate([sub[:, :HALF], sub[:, HALF:]], axis=0).astype(f32)
    packed[...] = natural.T.astype(bf16)
    for q in range(PAIRS):
        field1[PAIRS * r + q] = jnp.zeros((BLK, LANES), bf16)
    pl.semaphore_wait(barrier, COLS - 1 + 2 * (ROWS - 1))

    sends = []
    for d in range(1, COLS):
        to = lax.rem(c + d, COLS)
        copy = send(
            packed.at[pl.ds(pl.multiple_of(to * PIECE, PIECE), PIECE)], raw.at[c],
            out1.at[d], in1.at[c], r, to,
        )
        copy.start()
        sends.append(copy)
    raw[c] = packed[pl.ds(pl.multiple_of(c * PIECE, PIECE), PIECE), :]
    for d in range(1, COLS):
        src = lax.rem(c + d, COLS)
        send(packed.at[pl.ds(0, PIECE)], raw.at[src], out1.at[d], in1.at[src], r, src).wait_recv()
    rot_load.wait()
    left, right = [], []
    for e in range(COLS // 2):
        a, b = raw[2 * e].astype(f32), raw[2 * e + 1].astype(f32)
        left.append(jnp.where(lane == 0, a, swap_halves(b)))
        right.append(jnp.where(lane == 0, swap_halves(a), b))
    wide = jnp.concatenate(
        [jnp.concatenate(left, axis=1), jnp.concatenate(right, axis=1)], axis=0
    ).astype(bf16)
    rotated = jnp.dot(wide, rot[...], preferred_element_type=f32)
    for e in range(COLS // 2):
        a = rotated[:PIECE, e * LANES : (e + 1) * LANES]
        b = rotated[PIECE:, e * LANES : (e + 1) * LANES]
        mixed[2 * e] = jnp.where(lane == 0, a, swap_halves(b)).astype(bf16)
        mixed[2 * e + 1] = jnp.where(lane == 0, swap_halves(a), b).astype(bf16)

    def piece(of):
        return PAIRS * r + of // PAIRS, pl.ds(pl.multiple_of(lax.rem(of, PAIRS) * PIECE, PIECE), PIECE)

    for d in range(1, COLS):
        to = lax.rem(c + d, COLS)
        copy = send(mixed.at[to], field0.at[*piece(c)], out2.at[d], in2.at[c], r, to)
        copy.start()
        sends.append(copy)
    field0[*piece(c)] = mixed[c]
    for d in range(1, COLS):
        src = lax.rem(c + d, COLS)
        send(mixed.at[0], field0.at[*piece(src)], out2.at[d], in2.at[src], r, src).wait_recv()
    for copy in sends:
        copy.wait_send()

    def chunk_rows(q):
        return pl.ds(pl.multiple_of(q * BLK, BLK), BLK)

    z, y = r // 2, lax.rem(r, 2)

    def at(dz, dy):
        return 2 * lax.rem(z + dz + 4, 4) + (lax.rem(y + dy, 2))

    whole_pair, low, high = (0, BLK), (0, BLK // 2), (BLK // 2, BLK // 2)
    by_z, by_y = (0, 128), (128, 64)
    FIRST = (
        ((0, 0), (1, 0), whole_pair),
        ((0, 0), (-1, 0), whole_pair),
        ((0, 0), (0, 1), whole_pair),
    )
    ONWARD = (
        (0, (-1, 0), (1, 0), low),
        (1, (1, 0), (-1, 0), high),
        (0, (-1, 0), (1, 1), low),
        (1, (1, 0), (-1, 1), high),
        (0, (-1, 0), (0, 1), by_y),
        (1, (1, 0), (0, 1), by_y),
        (2, (0, 1), (1, 0), by_z),
        (2, (0, 1), (-1, 0), by_z),
    )

    def row_copy(par, q, n, src, to, part):
        view = fields[par].at[PAIRS * at(*src) + q, pl.ds(part[0], part[1])]
        return send(view, view, row_out.at[q, n], row_in.at[par, q, n], at(*to), c)

    def arrival(par, q, n, src, to, part):
        return row_copy(par, q, n, (src[0] - to[0], src[1] + to[1]), to, part)

    def spread(par, q):
        for n, (src, to, part) in enumerate(FIRST):
            row_copy(par, q, n, src, to, part).start()

    def onward(par, q):
        for n, (src, to, part) in enumerate(FIRST):
            arrival(par, q, n, src, to, part).wait_recv()
            for m, (after, src2, to2, part2) in enumerate(ONWARD):
                if after == n:
                    row_copy(par, q, 3 + m, src2, to2, part2).start()

    def await_all(par):
        def step(q, carry):
            for n, (src, to, part) in enumerate(FIRST):
                row_copy(par, q, n, src, to, part).wait_send()
            for m, (_, src, to, part) in enumerate(ONWARD):
                arrival(par, q, 3 + m, src, to, part).wait_recv()
                row_copy(par, q, 3 + m, src, to, part).wait_send()
            return carry

        lax.fori_loop(0, PAIRS, step, 0)

    def block_row(par, i):
        total = jnp.zeros((BLK, LANES), f32)
        for s in range(SLOTS):
            col = cols[i, s]
            part = fields[par][((col >> 3) << 2) + (col & 3)]
            part = jnp.where(lane == ((col >> 2) & 1), part, jnp.zeros_like(part))
            total += jnp.dot(tiles[i, s], part, preferred_element_type=f32)
        return total + swap_halves(total)

    def applied(par, q):
        return jnp.where(lane == 0, block_row(par, q), block_row(par, q + PAIRS))

    def next_level(par, q, scale):
        now = fields[par][PAIRS * r + q].astype(f32)
        before = fields[1 - par][PAIRS * r + q].astype(f32)
        level = scale * (applied(par, q) - CENTER * now) - before
        fields[1 - par][PAIRS * r + q] = level.astype(bf16)

    for q in range(PAIRS):
        spread(0, q)
    for q in range(PAIRS):
        onward(0, q)
    for load in loads:
        load.wait()

    def sib_copy(which, q):
        src = fields[which].at[PAIRS * r + q]
        return send(
            src, peer.at[which, q], sib_out.at[which, q], sib_in.at[which, q], r, sibling
        )

    def merged_pair(which, q):
        own = fields[which][PAIRS * r + q].astype(f32)
        other = swap_halves(peer[which, q].astype(f32))
        return jnp.where(lane == core, own, other)

    high_y, x = chip // 4, lax.rem(chip, 4)
    ACROSS = ((1, 0), (3, 0), (2, 0))
    COL = ((0, 1), *ACROSS)

    def chip_at(dx, dy):
        return 4 * lax.rem(high_y + dy, 2) + lax.rem(x + dx, 4)

    def col_copy(q, n, source_chip, to):
        view = every.at[source_chip, q]
        return send(view, view, col_out.at[q, n], col_in.at[q, n], r, 2 * to + core)

    def col_first(q):
        sib_copy(0, q).wait()
        every[chip, q] = merged_pair(0, q).astype(bf16)
        for n, to in enumerate(COL):
            col_copy(q, n, chip, chip_at(*to)).start()

    def col_onward(q):
        other = chip_at(0, 1)
        col_copy(q, 0, other, other).wait_recv()
        for n, to in enumerate(ACROSS):
            col_copy(q, 4 + n, other, chip_at(*to)).start()

    def col_await():
        def step(q, carry):
            other = chip_at(0, 1)
            col_copy(q, 0, chip, other).wait_send()
            for n, to in enumerate(ACROSS):
                col_copy(q, 1 + n, chip, chip_at(*to)).wait_send()
                col_copy(q, 4 + n, other, chip_at(*to)).wait_send()
                col_copy(q, 1 + n, chip_at(4 - to[0], 0), chip_at(*to)).wait_recv()
                col_copy(q, 4 + n, chip_at(4 - to[0], 1), chip_at(*to)).wait_recv()
            return carry

        lax.fori_loop(0, PAIRS, step, 0)

    def one_level(par, scale, last):
        await_all(par)

        def pair(q, carry):
            next_level(par, q, scale)
            spread(1 - par, q)
            if last is not None:

                @pl.when(last)
                def _():
                    sib_copy(0, q).start()

                    @pl.when(q >= 1)
                    def _():
                        col_first(q - 1)

            @pl.when(q >= LAG)
            def _():
                onward(1 - par, q - LAG)

            return carry

        lax.fori_loop(0, PAIRS, pair, 0)
        if last is not None:

            @pl.when(last)
            def _():
                col_first(PAIRS - 1)

        for q in range(PAIRS - LAG, PAIRS):
            onward(1 - par, q)

    def two_levels(k, carry):
        one_level(0, jnp.where(k == 0, 1.0 / WIDTH, 2.0 / WIDTH), None)
        one_level(1, 2.0 / WIDTH, k == DEGREE // 2 - 1)
        return carry

    lax.fori_loop(0, DEGREE // 2, two_levels, 0)

    lax.fori_loop(0, PAIRS, lambda q, carry: (col_onward(q), carry)[1], 0)
    flat = jnp.concatenate([field0[PAIRS * r + q] for q in range(PAIRS)], axis=0)
    flat = flat.astype(f32).T.astype(bf16)
    filt[:, :HALF] = flat[: LANES // 2]
    filt[:, HALF:] = flat[LANES // 2 :]
    own_half = every[chip].reshape(HALF, LANES).astype(f32).T.astype(bf16)
    await_all(0)

    source = 2 * r + core

    def sum_copy(w, n, to_row, to_core, src):
        return send(
            terms.at[w, to_row, to_core], parts.at[w, src], sum_out.at[w, n], sum_in.at[w, src],
            to_row, 2 * chip + to_core,
        )

    def member(n):
        index = lax.rem(source + n, 2 * ROWS)
        return index // 2, lax.rem(index, 2), index

    def send_terms(w, modes):
        for e in range(ROWS):
            product = jnp.dot(
                modes, every[e].reshape(HALF, LANES), preferred_element_type=f32
            ).astype(bf16)
            terms[w, e, 0] = product[: LANES // 2]
            terms[w, e, 1] = product[LANES // 2 :]
        for n in range(1, 2 * ROWS):
            to_row, to_core, _ = member(n)
            sum_copy(w, n, to_row, to_core, source).start()
        parts[w, source] = terms[w, r, core]

    def add_terms(w):
        for n in range(1, 2 * ROWS):
            to_row, to_core, index = member(n)
            sum_copy(w, n, r, core, index).wait_recv()
            sum_copy(w, n, to_row, to_core, source).wait_send()
        total = parts[w, 0].astype(f32)
        for n in range(1, 2 * ROWS):
            total += parts[w, n].astype(f32)
        return total * (1.0 / (ROWS * 2 * HALF))

    def image_pair(q):
        field1[PAIRS * r + q] = applied(0, q).astype(bf16)
        sib_copy(1, q).start()

    def image_step(q, carry):
        image_pair(q)

        @pl.when(q == PAIRS - 2)
        def _():
            col_await()
            send_terms(0, own_half)

        return carry

    lax.fori_loop(0, PAIRS, image_step, 0)
    halves = []
    for q in range(PAIRS):
        sib_copy(1, q).wait()
        halves.append(merged_pair(1, q))
    send_terms(1, jnp.concatenate(halves, axis=0).T.astype(bf16))
    gram[...] = add_terms(0)
    ray[...] = add_terms(1)


def copy_out(filt, gram, ray, filt_out, gram_out, ray_out, sems):
    copies = [
        pltpu.make_async_copy(src, dst, sems.at[n])
        for n, (src, dst) in enumerate(((filt, filt_out), (gram, gram_out), (ray, ray_out)))
    ]
    for copy in copies:
        copy.start()
    for copy in copies:
        copy.wait()


def local(subspace, rotation, block_tiles, block_cols):
    bf16, f32 = jnp.bfloat16, jnp.float32
    vmem = pl.BlockSpec(memory_space=pltpu.VMEM)
    dma = pltpu.SemaphoreType.DMA
    results = pl.pallas_call(
        kernel,
        out_shape=(
            jax.ShapeDtypeStruct(subspace.shape, bf16),
            jax.ShapeDtypeStruct((LANES // 2, LANES), f32),
            jax.ShapeDtypeStruct((LANES // 2, LANES), f32),
        ),
        in_specs=[
            pl.BlockSpec(memory_space=pltpu.SMEM),
            vmem,
            pl.BlockSpec(memory_space=pl.ANY),
            pl.BlockSpec(memory_space=pl.ANY),
        ],
        out_specs=(vmem, vmem, vmem),
        scratch_shapes=[
            pltpu.VMEM((ROWS * PAIRS, BLK, LANES), bf16),
            pltpu.VMEM((ROWS * PAIRS, BLK, LANES), bf16),
            pltpu.VMEM(block_tiles.shape, bf16),
            pltpu.VMEM(rotation.shape, bf16),
            pltpu.VMEM((HALF, LANES), bf16),
            pltpu.VMEM((COLS, PIECE, LANES), bf16),
            pltpu.VMEM((COLS, PIECE, LANES), bf16),
            pltpu.VMEM((2, PAIRS, BLK, LANES), bf16),
            pltpu.VMEM((ROWS, PAIRS, BLK, LANES), bf16),
            pltpu.VMEM((2, ROWS, 2, LANES // 2, LANES), bf16),
            pltpu.VMEM((2, 2 * ROWS, LANES // 2, LANES), bf16),
            dma((8,)),
            dma,
            dma((COLS,)),
            dma((COLS,)),
            dma((COLS,)),
            dma((COLS,)),
            dma((PAIRS, 11)),
            dma((2, PAIRS, 11)),
            dma((2, PAIRS)),
            dma((2, PAIRS)),
            dma((PAIRS, 7)),
            dma((PAIRS, 7)),
            dma((2, 2 * ROWS)),
            dma((2, 2 * ROWS)),
        ],
        compiler_params=pltpu.CompilerParams(
            collective_id=0, has_side_effects=True, vmem_limit_bytes=56 * 2**20
        ),
        cost_estimate=pl.CostEstimate(flops=7_000_000_000, bytes_accessed=30_000_000, transcendentals=0),
    )(block_cols, subspace, rotation, block_tiles)
    anywhere = pl.BlockSpec(memory_space=pl.ANY)
    return pl.pallas_call(
        copy_out,
        out_shape=tuple(jax.ShapeDtypeStruct(x.shape, x.dtype) for x in results),
        in_specs=[anywhere] * 3,
        out_specs=(anywhere,) * 3,
        scratch_shapes=[dma((3,))],
    )(*results)


def solution(mesh):
    return jax.shard_map(
        local,
        mesh=mesh,
        in_specs=(P("col", "row"), P(), P("row", None, None, None), P("row", None)),
        out_specs=(P("col", "row"), P("col", "row"), P("col", "row")),
        check_vma=False,
    )
```

```python
import functools

import jax
import jax.numpy as jnp
from jax import lax
from jax.experimental import pallas as pl
from jax.experimental.pallas import tpu as pltpu
from jax.sharding import PartitionSpec as P

MESH = pl.DeviceIdType.MESH
DEGREE = 4
CENTER = 1.6
WIDTH = 0.9
ROWS = 8
COLS = 16
BLK = 192
SLOTS = 31
PAIRS = 4
HALF = PAIRS * BLK
PIECE = HALF // COLS
GROUP = 2
LAG = 3
LANES = 128


def swap_halves(values):
    return pltpu.roll(values, LANES // 2, 1)


def kernel(
    cols, sub, rot_hbm, tiles_hbm, filt, gram, ray,
    field0, field1, tiles, rot, packed, raw, mixed, peer, every, terms, parts,
    load_sem, rot_sem, out1, in1, out2, in2, row_out, row_in,
    sib_out, sib_in, col_out, col_in, sum_out, sum_in,
):
    r = lax.axis_index("row")
    c = lax.axis_index("col")
    core = lax.rem(c, 2)
    chip = c // 2
    sibling = c + 1 - 2 * core
    f32, bf16 = jnp.float32, jnp.bfloat16
    fields = (field0, field1)
    lane = lax.broadcasted_iota(jnp.int32, (1, LANES), 1) // (LANES // 2)

    loads = [pltpu.make_async_copy(tiles_hbm.at[i], tiles.at[i], load_sem.at[i]) for i in range(8)]
    rot_load = pltpu.make_async_copy(rot_hbm, rot, rot_sem)
    rot_load.start()
    for load in loads:
        load.start()

    def send(src, dst, out_sem, in_sem, to_row, to_col):
        copy = pltpu.make_async_remote_copy(
            src_ref=src, dst_ref=dst, send_sem=out_sem, recv_sem=in_sem,
            device_id=(to_row, to_col), device_id_type=MESH,
        )
        return copy

    barrier = pltpu.get_barrier_semaphore()
    for d in range(1, COLS):
        pl.semaphore_signal(barrier, inc=1, device_id=(r, lax.rem(c + d, COLS)), device_id_type=MESH)
    for d in range(1, ROWS):
        for k in (0, 1):
            pl.semaphore_signal(
                barrier, inc=1, device_id=(lax.rem(r + d, ROWS), 2 * chip + k), device_id_type=MESH
            )

    natural = jnp.concatenate([sub[:, :HALF], sub[:, HALF:]], axis=0).astype(f32)
    packed[...] = natural.T.astype(bf16)
    for q in range(PAIRS):
        field1[PAIRS * r + q] = jnp.zeros((BLK, LANES), bf16)
    pl.semaphore_wait(barrier, COLS - 1 + 2 * (ROWS - 1))

    sends = []
    for d in range(1, COLS):
        to = lax.rem(c + d, COLS)
        copy = send(
            packed.at[pl.ds(pl.multiple_of(to * PIECE, PIECE), PIECE)], raw.at[c],
            out1.at[d], in1.at[c], r, to,
        )
        copy.start()
        sends.append(copy)
    raw[c] = packed[pl.ds(pl.multiple_of(c * PIECE, PIECE), PIECE), :]
    for d in range(1, COLS):
        src = lax.rem(c + d, COLS)
        send(packed.at[pl.ds(0, PIECE)], raw.at[src], out1.at[d], in1.at[src], r, src).wait_recv()
    rot_load.wait()
    left, right = [], []
    for e in range(COLS // 2):
        a, b = raw[2 * e].astype(f32), raw[2 * e + 1].astype(f32)
        left.append(jnp.where(lane == 0, a, swap_halves(b)))
        right.append(jnp.where(lane == 0, swap_halves(a), b))
    wide = jnp.concatenate(
        [jnp.concatenate(left, axis=1), jnp.concatenate(right, axis=1)], axis=0
    ).astype(bf16)
    rotated = jnp.dot(wide, rot[...], preferred_element_type=f32)
    for e in range(COLS // 2):
        a = rotated[:PIECE, e * LANES : (e + 1) * LANES]
        b = rotated[PIECE:, e * LANES : (e + 1) * LANES]
        mixed[2 * e] = jnp.where(lane == 0, a, swap_halves(b)).astype(bf16)
        mixed[2 * e + 1] = jnp.where(lane == 0, swap_halves(a), b).astype(bf16)

    def piece(of):
        return PAIRS * r + of // PAIRS, pl.ds(pl.multiple_of(lax.rem(of, PAIRS) * PIECE, PIECE), PIECE)

    for d in range(1, COLS):
        to = lax.rem(c + d, COLS)
        copy = send(mixed.at[to], field0.at[*piece(c)], out2.at[d], in2.at[c], r, to)
        copy.start()
        sends.append(copy)
    field0[*piece(c)] = mixed[c]
    for d in range(1, COLS):
        src = lax.rem(c + d, COLS)
        send(mixed.at[0], field0.at[*piece(src)], out2.at[d], in2.at[src], r, src).wait_recv()
    for copy in sends:
        copy.wait_send()

    def chunk_rows(q):
        return pl.ds(pl.multiple_of(q * BLK, BLK), BLK)

    z, y = r // 2, lax.rem(r, 2)

    def at(dz, dy):
        return 2 * lax.rem(z + dz + 4, 4) + (lax.rem(y + dy, 2))

    whole_pair, low, high = (0, BLK), (0, BLK // 2), (BLK // 2, BLK // 2)
    by_z, by_y = (0, 128), (128, 64)
    FIRST = (
        ((0, 0), (1, 0), whole_pair),
        ((0, 0), (-1, 0), whole_pair),
        ((0, 0), (0, 1), whole_pair),
    )
    ONWARD = (
        (0, (-1, 0), (1, 0), low),
        (1, (1, 0), (-1, 0), high),
        (0, (-1, 0), (1, 1), low),
        (1, (1, 0), (-1, 1), high),
        (0, (-1, 0), (0, 1), by_y),
        (1, (1, 0), (0, 1), by_y),
        (2, (0, 1), (1, 0), by_z),
        (2, (0, 1), (-1, 0), by_z),
    )

    def row_copy(par, q, n, src, to, part):
        view = fields[par].at[PAIRS * at(*src) + q, pl.ds(part[0], part[1])]
        return send(view, view, row_out.at[q, n], row_in.at[par, q, n], at(*to), c)

    def arrival(par, q, n, src, to, part):
        return row_copy(par, q, n, (src[0] - to[0], src[1] + to[1]), to, part)

    def spread(par, q):
        for n, (src, to, part) in enumerate(FIRST):
            row_copy(par, q, n, src, to, part).start()

    def onward(par, q):
        for n, (src, to, part) in enumerate(FIRST):
            arrival(par, q, n, src, to, part).wait_recv()
            for m, (after, src2, to2, part2) in enumerate(ONWARD):
                if after == n:
                    row_copy(par, q, 3 + m, src2, to2, part2).start()

    def await_all(par):
        def step(q, carry):
            for n, (src, to, part) in enumerate(FIRST):
                row_copy(par, q, n, src, to, part).wait_send()
            for m, (_, src, to, part) in enumerate(ONWARD):
                arrival(par, q, 3 + m, src, to, part).wait_recv()
                row_copy(par, q, 3 + m, src, to, part).wait_send()
            return carry

        lax.fori_loop(0, PAIRS, step, 0)

    def picked(par, i, s):
        col = cols[i, s]
        part = fields[par][((col >> 3) << 2) + (col & 3)]
        return jnp.where(lane == ((col >> 2) & 1), part, jnp.zeros_like(part))

    def applied(par, q):
        totals = [jnp.zeros((BLK, LANES), f32)] * 2
        for s in range(0, SLOTS, GROUP):
            slots = range(s, min(s + GROUP, SLOTS))
            for n in range(2):
                i = q + PAIRS * n
                wide_tiles = jnp.concatenate([tiles[i, t] for t in slots], axis=1)
                blocks = jnp.concatenate([picked(par, i, t) for t in slots], axis=0)
                totals[n] += jnp.dot(wide_tiles, blocks, preferred_element_type=f32)
        first, second = totals
        return jnp.where(lane == 0, first + swap_halves(first), second + swap_halves(second))

    def next_level(par, q, scale):
        now = fields[par][PAIRS * r + q].astype(f32)
        before = fields[1 - par][PAIRS * r + q].astype(f32)
        level = scale * (applied(par, q) - CENTER * now) - before
        fields[1 - par][PAIRS * r + q] = level.astype(bf16)

    for q in range(PAIRS):
        spread(0, q)
    for q in range(PAIRS):
        onward(0, q)
    for load in loads:
        load.wait()

    def sib_copy(which, q):
        src = fields[which].at[PAIRS * r + q]
        return send(
            src, peer.at[which, q], sib_out.at[which, q], sib_in.at[which, q], r, sibling
        )

    def merged_pair(which, q):
        own = fields[which][PAIRS * r + q].astype(f32)
        other = swap_halves(peer[which, q].astype(f32))
        return jnp.where(lane == core, own, other)

    high_y, x = chip // 4, lax.rem(chip, 4)
    ACROSS = ((1, 0), (3, 0), (2, 0))
    COL = ((0, 1), *ACROSS)

    def chip_at(dx, dy):
        return 4 * lax.rem(high_y + dy, 2) + lax.rem(x + dx, 4)

    def col_copy(q, n, source_chip, to):
        view = every.at[source_chip, q]
        return send(view, view, col_out.at[q, n], col_in.at[q, n], r, 2 * to + core)

    def col_first(q):
        sib_copy(0, q).wait()
        every[chip, q] = merged_pair(0, q).astype(bf16)
        for n, to in enumerate(COL):
            col_copy(q, n, chip, chip_at(*to)).start()

    def col_onward(q):
        other = chip_at(0, 1)
        col_copy(q, 0, other, other).wait_recv()
        for n, to in enumerate(ACROSS):
            col_copy(q, 4 + n, other, chip_at(*to)).start()

    def col_await():
        def step(q, carry):
            other = chip_at(0, 1)
            col_copy(q, 0, chip, other).wait_send()
            for n, to in enumerate(ACROSS):
                col_copy(q, 1 + n, chip, chip_at(*to)).wait_send()
                col_copy(q, 4 + n, other, chip_at(*to)).wait_send()
                col_copy(q, 1 + n, chip_at(4 - to[0], 0), chip_at(*to)).wait_recv()
                col_copy(q, 4 + n, chip_at(4 - to[0], 1), chip_at(*to)).wait_recv()
            return carry

        lax.fori_loop(0, PAIRS, step, 0)

    def one_level(par, scale, last):
        await_all(par)

        def pair(q, carry):
            next_level(par, q, scale)
            spread(1 - par, q)
            if last is not None:

                @pl.when(last)
                def _():
                    sib_copy(0, q).start()

                    @pl.when(q >= 1)
                    def _():
                        col_first(q - 1)

            @pl.when(q >= LAG)
            def _():
                onward(1 - par, q - LAG)

            return carry

        lax.fori_loop(0, PAIRS, pair, 0)
        if last is not None:

            @pl.when(last)
            def _():
                col_first(PAIRS - 1)

        for q in range(PAIRS - LAG, PAIRS):
            onward(1 - par, q)

    def two_levels(k, carry):
        one_level(0, jnp.where(k == 0, 1.0 / WIDTH, 2.0 / WIDTH), None)
        one_level(1, 2.0 / WIDTH, k == DEGREE // 2 - 1)
        return carry

    lax.fori_loop(0, DEGREE // 2, two_levels, 0)

    lax.fori_loop(0, PAIRS, lambda q, carry: (col_onward(q), carry)[1], 0)
    flat = jnp.concatenate([field0[PAIRS * r + q] for q in range(PAIRS)], axis=0)
    flat = flat.astype(f32).T.astype(bf16)
    filt[:, :HALF] = flat[: LANES // 2]
    filt[:, HALF:] = flat[LANES // 2 :]
    own_half = every[chip].reshape(HALF, LANES).astype(f32).T.astype(bf16)
    await_all(0)

    source = 2 * r + core

    def sum_copy(w, n, to_row, to_core, src):
        return send(
            terms.at[w, to_row, to_core], parts.at[w, src], sum_out.at[w, n], sum_in.at[w, src],
            to_row, 2 * chip + to_core,
        )

    def member(n):
        index = lax.rem(source + n, 2 * ROWS)
        return index // 2, lax.rem(index, 2), index

    def send_terms(w, modes):
        for e in range(ROWS):
            product = jnp.dot(
                modes, every[e].reshape(HALF, LANES), preferred_element_type=f32
            ).astype(bf16)
            terms[w, e, 0] = product[: LANES // 2]
            terms[w, e, 1] = product[LANES // 2 :]
        for n in range(1, 2 * ROWS):
            to_row, to_core, _ = member(n)
            sum_copy(w, n, to_row, to_core, source).start()
        parts[w, source] = terms[w, r, core]

    def add_terms(w):
        for n in range(1, 2 * ROWS):
            to_row, to_core, index = member(n)
            sum_copy(w, n, r, core, index).wait_recv()
            sum_copy(w, n, to_row, to_core, source).wait_send()
        total = parts[w, 0].astype(f32)
        for n in range(1, 2 * ROWS):
            total += parts[w, n].astype(f32)
        return total * (1.0 / (ROWS * 2 * HALF))

    def image_pair(q):
        field1[PAIRS * r + q] = applied(0, q).astype(bf16)
        sib_copy(1, q).start()

    def image_step(q, carry):
        image_pair(q)

        @pl.when(q == PAIRS - 2)
        def _():
            col_await()
            send_terms(0, own_half)

        return carry

    lax.fori_loop(0, PAIRS, image_step, 0)
    halves = []
    for q in range(PAIRS):
        sib_copy(1, q).wait()
        halves.append(merged_pair(1, q))
    send_terms(1, jnp.concatenate(halves, axis=0).T.astype(bf16))
    gram[...] = add_terms(0)
    ray[...] = add_terms(1)


def copy_out(filt, gram, ray, filt_out, gram_out, ray_out):
    filt_out[...] = filt[...]
    gram_out[...] = gram[...]
    ray_out[...] = ray[...]


def local(subspace, rotation, block_tiles, block_cols):
    bf16, f32 = jnp.bfloat16, jnp.float32
    vmem = pl.BlockSpec(memory_space=pltpu.VMEM)
    dma = pltpu.SemaphoreType.DMA
    results = pl.pallas_call(
        kernel,
        out_shape=(
            jax.ShapeDtypeStruct(subspace.shape, bf16),
            jax.ShapeDtypeStruct((LANES // 2, LANES), f32),
            jax.ShapeDtypeStruct((LANES // 2, LANES), f32),
        ),
        in_specs=[
            pl.BlockSpec(memory_space=pltpu.SMEM),
            vmem,
            pl.BlockSpec(memory_space=pl.ANY),
            pl.BlockSpec(memory_space=pl.ANY),
        ],
        out_specs=(vmem, vmem, vmem),
        scratch_shapes=[
            pltpu.VMEM((ROWS * PAIRS, BLK, LANES), bf16),
            pltpu.VMEM((ROWS * PAIRS, BLK, LANES), bf16),
            pltpu.VMEM(block_tiles.shape, bf16),
            pltpu.VMEM(rotation.shape, bf16),
            pltpu.VMEM((HALF, LANES), bf16),
            pltpu.VMEM((COLS, PIECE, LANES), bf16),
            pltpu.VMEM((COLS, PIECE, LANES), bf16),
            pltpu.VMEM((2, PAIRS, BLK, LANES), bf16),
            pltpu.VMEM((ROWS, PAIRS, BLK, LANES), bf16),
            pltpu.VMEM((2, ROWS, 2, LANES // 2, LANES), bf16),
            pltpu.VMEM((2, 2 * ROWS, LANES // 2, LANES), bf16),
            dma((8,)),
            dma,
            dma((COLS,)),
            dma((COLS,)),
            dma((COLS,)),
            dma((COLS,)),
            dma((PAIRS, 11)),
            dma((2, PAIRS, 11)),
            dma((2, PAIRS)),
            dma((2, PAIRS)),
            dma((PAIRS, 7)),
            dma((PAIRS, 7)),
            dma((2, 2 * ROWS)),
            dma((2, 2 * ROWS)),
        ],
        compiler_params=pltpu.CompilerParams(
            collective_id=0, has_side_effects=True, vmem_limit_bytes=56 * 2**20
        ),
        cost_estimate=pl.CostEstimate(flops=7_000_000_000, bytes_accessed=30_000_000, transcendentals=0),
    )(block_cols, subspace, rotation, block_tiles)
    return pl.pallas_call(
        copy_out,
        out_shape=tuple(jax.ShapeDtypeStruct(x.shape, x.dtype) for x in results),
        in_specs=[vmem] * 3,
        out_specs=(vmem,) * 3,
    )(*results)


def solution(mesh):
    return jax.shard_map(
        local,
        mesh=mesh,
        in_specs=(P("col", "row"), P(), P("row", None, None, None), P("row", None)),
        out_specs=(P("col", "row"), P("col", "row"), P("col", "row")),
        check_vma=False,
    )
```

```python
import functools

import jax
import jax.numpy as jnp
from jax import lax
from jax.experimental import pallas as pl
from jax.experimental.pallas import tpu as pltpu
from jax.sharding import PartitionSpec as P

MESH = pl.DeviceIdType.MESH
DEGREE = 4
CENTER = 1.6
WIDTH = 0.9
ROWS = 8
COLS = 16
BLK = 192
SLOTS = 31
PAIRS = 4
HALF = PAIRS * BLK
PIECE = HALF // COLS
GROUP = 2
THREE_LEGS = 2
LANES = 128


def swap_halves(values):
    return pltpu.roll(values, LANES // 2, 1)


def kernel(
    cols, sub, rot_hbm, tiles_hbm, filt, gram, ray,
    field0, field1, tiles, rot, packed, raw, mixed, peer, every, terms, parts,
    load_sem, rot_sem, out1, in1, out2, in2, row_out, row_in,
    sib_out, sib_in, col_out, col_in, sum_out, sum_in,
):
    r = lax.axis_index("row")
    c = lax.axis_index("col")
    core = lax.rem(c, 2)
    chip = c // 2
    sibling = c + 1 - 2 * core
    f32, bf16 = jnp.float32, jnp.bfloat16
    fields = (field0, field1)
    lane = lax.broadcasted_iota(jnp.int32, (1, LANES), 1) // (LANES // 2)

    loads = [pltpu.make_async_copy(tiles_hbm.at[i], tiles.at[i], load_sem.at[i]) for i in range(8)]
    rot_load = pltpu.make_async_copy(rot_hbm, rot, rot_sem)
    rot_load.start()
    for load in loads:
        load.start()

    def send(src, dst, out_sem, in_sem, to_row, to_col):
        copy = pltpu.make_async_remote_copy(
            src_ref=src, dst_ref=dst, send_sem=out_sem, recv_sem=in_sem,
            device_id=(to_row, to_col), device_id_type=MESH,
        )
        return copy

    barrier = pltpu.get_barrier_semaphore()
    for d in range(1, COLS):
        pl.semaphore_signal(barrier, inc=1, device_id=(r, lax.rem(c + d, COLS)), device_id_type=MESH)
    for d in range(1, ROWS):
        for k in (0, 1):
            pl.semaphore_signal(
                barrier, inc=1, device_id=(lax.rem(r + d, ROWS), 2 * chip + k), device_id_type=MESH
            )

    natural = jnp.concatenate([sub[:, :HALF], sub[:, HALF:]], axis=0).astype(f32)
    packed[...] = natural.T.astype(bf16)
    for q in range(PAIRS):
        field1[PAIRS * r + q] = jnp.zeros((BLK, LANES), bf16)
    pl.semaphore_wait(barrier, COLS - 1 + 2 * (ROWS - 1))

    sends = []
    for d in range(1, COLS):
        to = lax.rem(c + d, COLS)
        copy = send(
            packed.at[pl.ds(pl.multiple_of(to * PIECE, PIECE), PIECE)], raw.at[c],
            out1.at[d], in1.at[c], r, to,
        )
        copy.start()
        sends.append(copy)
    raw[c] = packed[pl.ds(pl.multiple_of(c * PIECE, PIECE), PIECE), :]
    for d in range(1, COLS):
        src = lax.rem(c + d, COLS)
        send(packed.at[pl.ds(0, PIECE)], raw.at[src], out1.at[d], in1.at[src], r, src).wait_recv()
    rot_load.wait()
    left, right = [], []
    for e in range(COLS // 2):
        a, b = raw[2 * e].astype(f32), raw[2 * e + 1].astype(f32)
        left.append(jnp.where(lane == 0, a, swap_halves(b)))
        right.append(jnp.where(lane == 0, swap_halves(a), b))
    wide = jnp.concatenate(
        [jnp.concatenate(left, axis=1), jnp.concatenate(right, axis=1)], axis=0
    ).astype(bf16)
    rotated = jnp.dot(wide, rot[...], preferred_element_type=f32)
    for e in range(COLS // 2):
        a = rotated[:PIECE, e * LANES : (e + 1) * LANES]
        b = rotated[PIECE:, e * LANES : (e + 1) * LANES]
        mixed[2 * e] = jnp.where(lane == 0, a, swap_halves(b)).astype(bf16)
        mixed[2 * e + 1] = jnp.where(lane == 0, swap_halves(a), b).astype(bf16)

    def piece(of):
        return PAIRS * r + of // PAIRS, pl.ds(pl.multiple_of(lax.rem(of, PAIRS) * PIECE, PIECE), PIECE)

    for d in range(1, COLS):
        to = lax.rem(c + d, COLS)
        copy = send(mixed.at[to], field0.at[*piece(c)], out2.at[d], in2.at[c], r, to)
        copy.start()
        sends.append(copy)
    field0[*piece(c)] = mixed[c]
    for d in range(1, COLS):
        src = lax.rem(c + d, COLS)
        send(mixed.at[0], field0.at[*piece(src)], out2.at[d], in2.at[src], r, src).wait_recv()
    for copy in sends:
        copy.wait_send()

    def chunk_rows(q):
        return pl.ds(pl.multiple_of(q * BLK, BLK), BLK)

    z, y = r // 2, lax.rem(r, 2)

    def at(dz, dy):
        return 2 * lax.rem(z + dz + 4, 4) + (lax.rem(y + dy, 2))

    whole_pair, low, high = (0, BLK), (0, BLK // 2), (BLK // 2, BLK // 2)
    FIRST = (
        ((0, 0), (1, 0), whole_pair),
        ((0, 0), (-1, 0), whole_pair),
        ((0, 0), (0, 1), whole_pair),
    )

    def onward_plan(q):
        split = 160 if q < THREE_LEGS else 128
        by_z, by_y = (0, split), (split, BLK - split)
        plan = (
            (0, (-1, 0), (1, 0), low),
            (1, (1, 0), (-1, 0), high),
            (0, (-1, 0), (0, 1), by_y),
            (1, (1, 0), (0, 1), by_y),
            (2, (0, 1), (1, 0), by_z),
            (2, (0, 1), (-1, 0), by_z),
        )
        far = ((0, (-1, 0), (1, 1), low), (1, (1, 0), (-1, 1), high))
        return plan, far

    THIRD = (((2, 0), (0, 1), low), ((2, 0), (0, 1), high))

    def row_copy(par, q, n, src, to, part):
        view = fields[par].at[PAIRS * at(*src) + q, pl.ds(part[0], part[1])]
        return send(view, view, row_out.at[q, n], row_in.at[par, q, n], at(*to), c)

    def arrival(par, q, n, src, to, part):
        return row_copy(par, q, n, (src[0] - to[0], src[1] + to[1]), to, part)

    def spread(par, q):
        for n, (src, to, part) in enumerate(FIRST):
            row_copy(par, q, n, src, to, part).start()

    def onward(par, q):
        plan, far = onward_plan(q)
        steps = plan if q < THREE_LEGS else plan + far
        for n, (src, to, part) in enumerate(FIRST):
            arrival(par, q, n, src, to, part).wait_recv()
            for m, (after, src2, to2, part2) in enumerate(steps):
                if after == n:
                    row_copy(par, q, 3 + m, src2, to2, part2).start()

    def third(par, q):
        plan, _ = onward_plan(q)
        for m in range(2):
            arrival(par, q, 3 + m, *plan[m][1:]).wait_recv()
            row_copy(par, q, 9 + m, *THIRD[m]).start()

    def await_all(par):
        for q in range(PAIRS):
            plan, far = onward_plan(q)
            if q < THREE_LEGS:
                last = tuple((0, *step) for step in THIRD)
                pending = plan[2:] + last
            else:
                last = far
                pending = plan + last
            for n, (src, to, part) in enumerate(FIRST):
                row_copy(par, q, n, src, to, part).wait_send()
            for m, (_, src, to, part) in enumerate(plan + last):
                if (_, src, to, part) in pending:
                    arrival(par, q, 3 + m, src, to, part).wait_recv()
                row_copy(par, q, 3 + m, src, to, part).wait_send()

    def picked(par, i, s):
        col = cols[i, s]
        part = fields[par][((col >> 3) << 2) + (col & 3)]
        return jnp.where(lane == ((col >> 2) & 1), part, jnp.zeros_like(part))

    def applied(par, q):
        totals = [jnp.zeros((BLK, LANES), f32)] * 2
        for s in range(0, SLOTS, GROUP):
            slots = range(s, min(s + GROUP, SLOTS))
            for n in range(2):
                i = q + PAIRS * n
                wide_tiles = jnp.concatenate([tiles[i, t] for t in slots], axis=1)
                blocks = jnp.concatenate([picked(par, i, t) for t in slots], axis=0)
                totals[n] += jnp.dot(wide_tiles, blocks, preferred_element_type=f32)
        first, second = totals
        return jnp.where(lane == 0, first + swap_halves(first), second + swap_halves(second))

    def next_level(par, q, scale):
        now = fields[par][PAIRS * r + q].astype(f32)
        before = fields[1 - par][PAIRS * r + q].astype(f32)
        level = scale * (applied(par, q) - CENTER * now) - before
        fields[1 - par][PAIRS * r + q] = level.astype(bf16)

    for q in range(PAIRS):
        spread(0, q)
    for q in range(PAIRS):
        onward(0, q)
    for q in range(THREE_LEGS):
        third(0, q)
    for load in loads:
        load.wait()

    def sib_copy(which, q):
        src = fields[which].at[PAIRS * r + q]
        return send(
            src, peer.at[which, q], sib_out.at[which, q], sib_in.at[which, q], r, sibling
        )

    def merged_pair(which, q):
        own = fields[which][PAIRS * r + q].astype(f32)
        other = swap_halves(peer[which, q].astype(f32))
        return jnp.where(lane == core, own, other)

    high_y, x = chip // 4, lax.rem(chip, 4)
    ACROSS = ((1, 0), (3, 0), (2, 0))
    COL = ((0, 1), *ACROSS)

    def chip_at(dx, dy):
        return 4 * lax.rem(high_y + dy, 2) + lax.rem(x + dx, 4)

    def col_copy(q, n, source_chip, to):
        view = every.at[source_chip, q]
        return send(view, view, col_out.at[q, n], col_in.at[q, n], r, 2 * to + core)

    def col_first(q):
        sib_copy(0, q).wait()
        every[chip, q] = merged_pair(0, q).astype(bf16)
        for n, to in enumerate(COL):
            col_copy(q, n, chip, chip_at(*to)).start()

    def col_onward(q):
        other = chip_at(0, 1)
        col_copy(q, 0, other, other).wait_recv()
        for n, to in enumerate(ACROSS):
            col_copy(q, 4 + n, other, chip_at(*to)).start()

    def col_await():
        def step(q, carry):
            other = chip_at(0, 1)
            col_copy(q, 0, chip, other).wait_send()
            for n, to in enumerate(ACROSS):
                col_copy(q, 1 + n, chip, chip_at(*to)).wait_send()
                col_copy(q, 4 + n, other, chip_at(*to)).wait_send()
                col_copy(q, 1 + n, chip_at(4 - to[0], 0), chip_at(*to)).wait_recv()
                col_copy(q, 4 + n, chip_at(4 - to[0], 1), chip_at(*to)).wait_recv()
            return carry

        lax.fori_loop(0, PAIRS, step, 0)

    def one_level(par, scale, last):
        await_all(par)

        def pair(q, carry):
            next_level(par, q, scale)
            spread(1 - par, q)
            if last is not None:

                @pl.when(last)
                def _():
                    sib_copy(0, q).start()

                    @pl.when(q >= 1)
                    def _():
                        col_first(q - 1)

            return carry

        lax.fori_loop(0, PAIRS, pair, 0)
        if last is not None:

            @pl.when(last)
            def _():
                col_first(PAIRS - 1)

        for q in range(PAIRS):
            onward(1 - par, q)
        for q in range(THREE_LEGS):
            third(1 - par, q)

    def two_levels(k, carry):
        one_level(0, jnp.where(k == 0, 1.0 / WIDTH, 2.0 / WIDTH), None)
        one_level(1, 2.0 / WIDTH, k == DEGREE // 2 - 1)
        return carry

    lax.fori_loop(0, DEGREE // 2, two_levels, 0)

    lax.fori_loop(0, PAIRS, lambda q, carry: (col_onward(q), carry)[1], 0)
    flat = jnp.concatenate([field0[PAIRS * r + q] for q in range(PAIRS)], axis=0)
    flat = flat.astype(f32).T.astype(bf16)
    filt[:, :HALF] = flat[: LANES // 2]
    filt[:, HALF:] = flat[LANES // 2 :]
    own_half = every[chip].reshape(HALF, LANES).astype(f32).T.astype(bf16)
    await_all(0)

    source = 2 * r + core

    def sum_copy(w, n, to_row, to_core, src):
        return send(
            terms.at[w, to_row, to_core], parts.at[w, src], sum_out.at[w, n], sum_in.at[w, src],
            to_row, 2 * chip + to_core,
        )

    def member(n):
        index = lax.rem(source + n, 2 * ROWS)
        return index // 2, lax.rem(index, 2), index

    def send_terms(w, modes):
        for e in range(ROWS):
            product = jnp.dot(
                modes, every[e].reshape(HALF, LANES), preferred_element_type=f32
            ).astype(bf16)
            terms[w, e, 0] = product[: LANES // 2]
            terms[w, e, 1] = product[LANES // 2 :]
        for n in range(1, 2 * ROWS):
            to_row, to_core, _ = member(n)
            sum_copy(w, n, to_row, to_core, source).start()
        parts[w, source] = terms[w, r, core]

    def add_terms(w):
        for n in range(1, 2 * ROWS):
            to_row, to_core, index = member(n)
            sum_copy(w, n, r, core, index).wait_recv()
            sum_copy(w, n, to_row, to_core, source).wait_send()
        total = parts[w, 0].astype(f32)
        for n in range(1, 2 * ROWS):
            total += parts[w, n].astype(f32)
        return total * (1.0 / (ROWS * 2 * HALF))

    def image_pair(q):
        field1[PAIRS * r + q] = applied(0, q).astype(bf16)
        sib_copy(1, q).start()

    def image_step(q, carry):
        image_pair(q)

        @pl.when(q == PAIRS - 2)
        def _():
            col_await()
            send_terms(0, own_half)

        return carry

    lax.fori_loop(0, PAIRS, image_step, 0)
    halves = []
    for q in range(PAIRS):
        sib_copy(1, q).wait()
        halves.append(merged_pair(1, q))
    send_terms(1, jnp.concatenate(halves, axis=0).T.astype(bf16))
    gram[...] = add_terms(0)
    ray[...] = add_terms(1)


def copy_out(filt, gram, ray, filt_out, gram_out, ray_out):
    filt_out[...] = filt[...]
    gram_out[...] = gram[...]
    ray_out[...] = ray[...]


def local(subspace, rotation, block_tiles, block_cols):
    bf16, f32 = jnp.bfloat16, jnp.float32
    vmem = pl.BlockSpec(memory_space=pltpu.VMEM)
    dma = pltpu.SemaphoreType.DMA
    results = pl.pallas_call(
        kernel,
        out_shape=(
            jax.ShapeDtypeStruct(subspace.shape, bf16),
            jax.ShapeDtypeStruct((LANES // 2, LANES), f32),
            jax.ShapeDtypeStruct((LANES // 2, LANES), f32),
        ),
        in_specs=[
            pl.BlockSpec(memory_space=pltpu.SMEM),
            vmem,
            pl.BlockSpec(memory_space=pl.ANY),
            pl.BlockSpec(memory_space=pl.ANY),
        ],
        out_specs=(vmem, vmem, vmem),
        scratch_shapes=[
            pltpu.VMEM((ROWS * PAIRS, BLK, LANES), bf16),
            pltpu.VMEM((ROWS * PAIRS, BLK, LANES), bf16),
            pltpu.VMEM(block_tiles.shape, bf16),
            pltpu.VMEM(rotation.shape, bf16),
            pltpu.VMEM((HALF, LANES), bf16),
            pltpu.VMEM((COLS, PIECE, LANES), bf16),
            pltpu.VMEM((COLS, PIECE, LANES), bf16),
            pltpu.VMEM((2, PAIRS, BLK, LANES), bf16),
            pltpu.VMEM((ROWS, PAIRS, BLK, LANES), bf16),
            pltpu.VMEM((2, ROWS, 2, LANES // 2, LANES), bf16),
            pltpu.VMEM((2, 2 * ROWS, LANES // 2, LANES), bf16),
            dma((8,)),
            dma,
            dma((COLS,)),
            dma((COLS,)),
            dma((COLS,)),
            dma((COLS,)),
            dma((PAIRS, 11)),
            dma((2, PAIRS, 11)),
            dma((2, PAIRS)),
            dma((2, PAIRS)),
            dma((PAIRS, 7)),
            dma((PAIRS, 7)),
            dma((2, 2 * ROWS)),
            dma((2, 2 * ROWS)),
        ],
        compiler_params=pltpu.CompilerParams(
            collective_id=0, has_side_effects=True, vmem_limit_bytes=56 * 2**20
        ),
        cost_estimate=pl.CostEstimate(flops=7_000_000_000, bytes_accessed=30_000_000, transcendentals=0),
    )(block_cols, subspace, rotation, block_tiles)
    return pl.pallas_call(
        copy_out,
        out_shape=tuple(jax.ShapeDtypeStruct(x.shape, x.dtype) for x in results),
        in_specs=[vmem] * 3,
        out_specs=(vmem,) * 3,
    )(*results)


def solution(mesh):
    return jax.shard_map(
        local,
        mesh=mesh,
        in_specs=(P("col", "row"), P(), P("row", None, None, None), P("row", None)),
        out_specs=(P("col", "row"), P("col", "row"), P("col", "row")),
        check_vma=False,
    )
```

```python
import functools

import jax
import jax.numpy as jnp
from jax import lax
from jax.experimental import pallas as pl
from jax.experimental.pallas import tpu as pltpu
from jax.sharding import PartitionSpec as P

MESH = pl.DeviceIdType.MESH
DEGREE = 4
CENTER = 1.6
WIDTH = 0.9
ROWS = 8
COLS = 16
BLK = 192
SLOTS = 31
PAIRS = 4
HALF = PAIRS * BLK
PIECE = HALF // COLS
GROUP = 2
THREE_LEGS = 2
LANES = 128


def swap_halves(values):
    return pltpu.roll(values, LANES // 2, 1)


def kernel(
    cols, sub, rot_hbm, tiles_hbm, filt, gram, ray,
    field0, field1, tiles, rot, packed, raw, mixed, peer, every, terms, parts,
    load_sem, rot_sem, out1, in1, out2, in2, row_out, row_in,
    sib_out, sib_in, col_out, col_in, sum_out, sum_in,
):
    r = lax.axis_index("row")
    c = lax.axis_index("col")
    core = lax.rem(c, 2)
    chip = c // 2
    sibling = c + 1 - 2 * core
    f32, bf16 = jnp.float32, jnp.bfloat16
    fields = (field0, field1)
    lane = lax.broadcasted_iota(jnp.int32, (1, LANES), 1) // (LANES // 2)

    loads = [pltpu.make_async_copy(tiles_hbm.at[i], tiles.at[i], load_sem.at[i]) for i in range(8)]
    rot_load = pltpu.make_async_copy(rot_hbm, rot, rot_sem)
    rot_load.start()
    for load in loads:
        load.start()

    def send(src, dst, out_sem, in_sem, to_row, to_col):
        copy = pltpu.make_async_remote_copy(
            src_ref=src, dst_ref=dst, send_sem=out_sem, recv_sem=in_sem,
            device_id=(to_row, to_col), device_id_type=MESH,
        )
        return copy

    far_steps = [
        (dy, dx, dk) for dy, dx in ((1, 2), (1, 1), (1, 3), (1, 0), (0, 2), (0, 1), (0, 3), (0, 0))
        for dk in (0, 1)
    ]
    far_steps.remove((0, 0, 0))

    def col_peer(d):
        dy, dx, dk = far_steps[d - 1]
        return 8 * lax.rem(c // 8 + dy, 2) + 2 * lax.rem(chip + dx, 4) + lax.rem(core + dk, 2)

    barrier = pltpu.get_barrier_semaphore()
    for d in range(1, COLS):
        pl.semaphore_signal(barrier, inc=1, device_id=(r, lax.rem(c + d, COLS)), device_id_type=MESH)
    for d in range(1, ROWS):
        for k in (0, 1):
            pl.semaphore_signal(
                barrier, inc=1, device_id=(lax.rem(r + d, ROWS), 2 * chip + k), device_id_type=MESH
            )

    natural = jnp.concatenate([sub[:, :HALF], sub[:, HALF:]], axis=0).astype(f32)
    packed[...] = natural.T.astype(bf16)
    for q in range(PAIRS):
        field1[PAIRS * r + q] = jnp.zeros((BLK, LANES), bf16)
    pl.semaphore_wait(barrier, COLS - 1 + 2 * (ROWS - 1))

    sends = []
    for d in range(1, COLS):
        to = col_peer(d)
        copy = send(
            packed.at[pl.ds(pl.multiple_of(to * PIECE, PIECE), PIECE)], raw.at[c],
            out1.at[d], in1.at[c], r, to,
        )
        copy.start()
        sends.append(copy)
    raw[c] = packed[pl.ds(pl.multiple_of(c * PIECE, PIECE), PIECE), :]
    for d in range(1, COLS):
        src = col_peer(COLS - d)
        send(packed.at[pl.ds(0, PIECE)], raw.at[src], out1.at[d], in1.at[src], r, src).wait_recv()
    rot_load.wait()
    left, right = [], []
    for e in range(COLS // 2):
        a, b = raw[2 * e].astype(f32), raw[2 * e + 1].astype(f32)
        left.append(jnp.where(lane == 0, a, swap_halves(b)))
        right.append(jnp.where(lane == 0, swap_halves(a), b))
    wide = jnp.concatenate(
        [jnp.concatenate(left, axis=1), jnp.concatenate(right, axis=1)], axis=0
    ).astype(bf16)
    rotated = jnp.dot(wide, rot[...], preferred_element_type=f32)
    for e in range(COLS // 2):
        a = rotated[:PIECE, e * LANES : (e + 1) * LANES]
        b = rotated[PIECE:, e * LANES : (e + 1) * LANES]
        mixed[2 * e] = jnp.where(lane == 0, a, swap_halves(b)).astype(bf16)
        mixed[2 * e + 1] = jnp.where(lane == 0, swap_halves(a), b).astype(bf16)

    def piece(of):
        return PAIRS * r + of // PAIRS, pl.ds(pl.multiple_of(lax.rem(of, PAIRS) * PIECE, PIECE), PIECE)

    for d in range(1, COLS):
        to = col_peer(d)
        copy = send(mixed.at[to], field0.at[*piece(c)], out2.at[d], in2.at[c], r, to)
        copy.start()
        sends.append(copy)
    field0[*piece(c)] = mixed[c]
    for d in range(1, COLS):
        src = col_peer(COLS - d)
        send(mixed.at[0], field0.at[*piece(src)], out2.at[d], in2.at[src], r, src).wait_recv()
    for copy in sends:
        copy.wait_send()

    def chunk_rows(q):
        return pl.ds(pl.multiple_of(q * BLK, BLK), BLK)

    z, y = r // 2, lax.rem(r, 2)

    def at(dz, dy):
        return 2 * lax.rem(z + dz + 4, 4) + (lax.rem(y + dy, 2))

    whole_pair, low, high = (0, BLK), (0, BLK // 2), (BLK // 2, BLK // 2)
    FIRST = (
        ((0, 0), (1, 0), whole_pair),
        ((0, 0), (-1, 0), whole_pair),
        ((0, 0), (0, 1), whole_pair),
    )

    def onward_plan(q):
        split = 160 if q < THREE_LEGS else 128
        by_z, by_y = (0, split), (split, BLK - split)
        plan = (
            (0, (-1, 0), (1, 0), low),
            (1, (1, 0), (-1, 0), high),
            (0, (-1, 0), (0, 1), by_y),
            (1, (1, 0), (0, 1), by_y),
            (2, (0, 1), (1, 0), by_z),
            (2, (0, 1), (-1, 0), by_z),
        )
        far = ((0, (-1, 0), (1, 1), low), (1, (1, 0), (-1, 1), high))
        return plan, far

    THIRD = (((2, 0), (0, 1), low), ((2, 0), (0, 1), high))

    def row_copy(par, q, n, src, to, part):
        view = fields[par].at[PAIRS * at(*src) + q, pl.ds(part[0], part[1])]
        return send(view, view, row_out.at[q, n], row_in.at[par, q, n], at(*to), c)

    def arrival(par, q, n, src, to, part):
        return row_copy(par, q, n, (src[0] - to[0], src[1] + to[1]), to, part)

    def spread(par, q):
        for n, (src, to, part) in enumerate(FIRST):
            row_copy(par, q, n, src, to, part).start()

    def onward(par, q):
        plan, far = onward_plan(q)
        steps = plan if q < THREE_LEGS else plan + far
        for n, (src, to, part) in enumerate(FIRST):
            arrival(par, q, n, src, to, part).wait_recv()
            for m, (after, src2, to2, part2) in enumerate(steps):
                if after == n:
                    row_copy(par, q, 3 + m, src2, to2, part2).start()

    def third(par, q):
        plan, _ = onward_plan(q)
        for m in range(2):
            arrival(par, q, 3 + m, *plan[m][1:]).wait_recv()
            row_copy(par, q, 9 + m, *THIRD[m]).start()

    def await_all(par):
        for q in range(PAIRS):
            plan, far = onward_plan(q)
            if q < THREE_LEGS:
                last = tuple((0, *step) for step in THIRD)
                pending = plan[2:] + last
            else:
                last = far
                pending = plan + last
            for n, (src, to, part) in enumerate(FIRST):
                row_copy(par, q, n, src, to, part).wait_send()
            for m, (_, src, to, part) in enumerate(plan + last):
                if (_, src, to, part) in pending:
                    arrival(par, q, 3 + m, src, to, part).wait_recv()
                row_copy(par, q, 3 + m, src, to, part).wait_send()

    def picked(par, i, s):
        col = cols[i, s]
        part = fields[par][((col >> 3) << 2) + (col & 3)]
        return jnp.where(lane == ((col >> 2) & 1), part, jnp.zeros_like(part))

    def applied(par, q):
        totals = [jnp.zeros((BLK, LANES), f32)] * 2
        for s in range(0, SLOTS, GROUP):
            slots = range(s, min(s + GROUP, SLOTS))
            for n in range(2):
                i = q + PAIRS * n
                wide_tiles = jnp.concatenate([tiles[i, t] for t in slots], axis=1)
                blocks = jnp.concatenate([picked(par, i, t) for t in slots], axis=0)
                totals[n] += jnp.dot(wide_tiles, blocks, preferred_element_type=f32)
        first, second = totals
        return jnp.where(lane == 0, first + swap_halves(first), second + swap_halves(second))

    def next_level(par, q, scale):
        now = fields[par][PAIRS * r + q].astype(f32)
        before = fields[1 - par][PAIRS * r + q].astype(f32)
        level = scale * (applied(par, q) - CENTER * now) - before
        fields[1 - par][PAIRS * r + q] = level.astype(bf16)

    for q in range(PAIRS):
        spread(0, q)
    for q in range(PAIRS):
        onward(0, q)
    for q in range(THREE_LEGS):
        third(0, q)
    for load in loads:
        load.wait()

    def sib_copy(which, q):
        src = fields[which].at[PAIRS * r + q]
        return send(
            src, peer.at[which, q], sib_out.at[which, q], sib_in.at[which, q], r, sibling
        )

    def merged_pair(which, q):
        own = fields[which][PAIRS * r + q].astype(f32)
        other = swap_halves(peer[which, q].astype(f32))
        return jnp.where(lane == core, own, other)

    high_y, x = chip // 4, lax.rem(chip, 4)
    ACROSS = ((1, 0), (3, 0), (2, 0))
    COL = ((0, 1), *ACROSS)

    def chip_at(dx, dy):
        return 4 * lax.rem(high_y + dy, 2) + lax.rem(x + dx, 4)

    def col_copy(q, n, source_chip, to):
        view = every.at[source_chip, q]
        return send(view, view, col_out.at[q, n], col_in.at[q, n], r, 2 * to + core)

    def col_first(q):
        sib_copy(0, q).wait()
        every[chip, q] = merged_pair(0, q).astype(bf16)
        for n, to in enumerate(COL):
            col_copy(q, n, chip, chip_at(*to)).start()

    def col_onward(q):
        other = chip_at(0, 1)
        col_copy(q, 0, other, other).wait_recv()
        for n, to in enumerate(ACROSS):
            col_copy(q, 4 + n, other, chip_at(*to)).start()

    def col_await():
        def step(q, carry):
            other = chip_at(0, 1)
            col_copy(q, 0, chip, other).wait_send()
            for n, to in enumerate(ACROSS):
                col_copy(q, 1 + n, chip, chip_at(*to)).wait_send()
                col_copy(q, 4 + n, other, chip_at(*to)).wait_send()
                col_copy(q, 1 + n, chip_at(4 - to[0], 0), chip_at(*to)).wait_recv()
                col_copy(q, 4 + n, chip_at(4 - to[0], 1), chip_at(*to)).wait_recv()
            return carry

        lax.fori_loop(0, PAIRS, step, 0)

    def one_level(par, scale, last):
        await_all(par)

        def pair(q, carry):
            next_level(par, q, scale)
            spread(1 - par, q)
            if last is not None:

                @pl.when(last)
                def _():
                    sib_copy(0, q).start()

                    @pl.when(q >= 1)
                    def _():
                        col_first(q - 1)

            return carry

        lax.fori_loop(0, PAIRS, pair, 0)
        if last is not None:

            @pl.when(last)
            def _():
                col_first(PAIRS - 1)

        for q in range(PAIRS):
            onward(1 - par, q)
        for q in range(THREE_LEGS):
            third(1 - par, q)

    def two_levels(k, carry):
        one_level(0, jnp.where(k == 0, 1.0 / WIDTH, 2.0 / WIDTH), None)
        one_level(1, 2.0 / WIDTH, k == DEGREE // 2 - 1)
        return carry

    lax.fori_loop(0, DEGREE // 2, two_levels, 0)

    lax.fori_loop(0, PAIRS, lambda q, carry: (col_onward(q), carry)[1], 0)
    flat = jnp.concatenate([field0[PAIRS * r + q] for q in range(PAIRS)], axis=0)
    flat = flat.astype(f32).T.astype(bf16)
    filt[:, :HALF] = flat[: LANES // 2]
    filt[:, HALF:] = flat[LANES // 2 :]
    own_half = every[chip].reshape(HALF, LANES).astype(f32).T.astype(bf16)
    await_all(0)

    source = 2 * r + core

    def sum_copy(w, n, to_row, to_core, src):
        return send(
            terms.at[w, to_row, to_core], parts.at[w, src], sum_out.at[w, n], sum_in.at[w, src],
            to_row, 2 * chip + to_core,
        )

    row_steps = [
        (dz, dy, dk) for dz, dy in ((2, 1), (1, 1), (-1, 1), (2, 0), (1, 0), (-1, 0), (0, 1), (0, 0))
        for dk in (0, 1)
    ]
    row_steps.remove((0, 0, 0))

    def member(n):
        dz, dy, dk = row_steps[n - 1]
        to_row, to_core = at(dz, dy), lax.rem(core + dk, 2)
        return to_row, to_core, 2 * to_row + to_core

    def send_terms(w, modes):
        for e in range(ROWS):
            product = jnp.dot(
                modes, every[e].reshape(HALF, LANES), preferred_element_type=f32
            ).astype(bf16)
            terms[w, e, 0] = product[: LANES // 2]
            terms[w, e, 1] = product[LANES // 2 :]
        for n in range(1, 2 * ROWS):
            to_row, to_core, _ = member(n)
            sum_copy(w, n, to_row, to_core, source).start()
        parts[w, source] = terms[w, r, core]

    def add_terms(w):
        for n in range(1, 2 * ROWS):
            to_row, to_core, index = member(n)
            sum_copy(w, n, r, core, index).wait_recv()
            sum_copy(w, n, to_row, to_core, source).wait_send()
        total = parts[w, 0].astype(f32)
        for n in range(1, 2 * ROWS):
            total += parts[w, n].astype(f32)
        return total * (1.0 / (ROWS * 2 * HALF))

    def image_pair(q):
        field1[PAIRS * r + q] = applied(0, q).astype(bf16)
        sib_copy(1, q).start()

    def image_step(q, carry):
        image_pair(q)

        @pl.when(q == PAIRS - 2)
        def _():
            col_await()
            send_terms(0, own_half)

        return carry

    lax.fori_loop(0, PAIRS, image_step, 0)
    halves = []
    for q in range(PAIRS):
        sib_copy(1, q).wait()
        halves.append(merged_pair(1, q))
    send_terms(1, jnp.concatenate(halves, axis=0).T.astype(bf16))
    gram[...] = add_terms(0)
    ray[...] = add_terms(1)


def copy_out(filt, gram, ray, filt_out, gram_out, ray_out):
    filt_out[...] = filt[...]
    gram_out[...] = gram[...]
    ray_out[...] = ray[...]


def local(subspace, rotation, block_tiles, block_cols):
    bf16, f32 = jnp.bfloat16, jnp.float32
    vmem = pl.BlockSpec(memory_space=pltpu.VMEM)
    dma = pltpu.SemaphoreType.DMA
    results = pl.pallas_call(
        kernel,
        out_shape=(
            jax.ShapeDtypeStruct(subspace.shape, bf16),
            jax.ShapeDtypeStruct((LANES // 2, LANES), f32),
            jax.ShapeDtypeStruct((LANES // 2, LANES), f32),
        ),
        in_specs=[
            pl.BlockSpec(memory_space=pltpu.SMEM),
            vmem,
            pl.BlockSpec(memory_space=pl.ANY),
            pl.BlockSpec(memory_space=pl.ANY),
        ],
        out_specs=(vmem, vmem, vmem),
        scratch_shapes=[
            pltpu.VMEM((ROWS * PAIRS, BLK, LANES), bf16),
            pltpu.VMEM((ROWS * PAIRS, BLK, LANES), bf16),
            pltpu.VMEM(block_tiles.shape, bf16),
            pltpu.VMEM(rotation.shape, bf16),
            pltpu.VMEM((HALF, LANES), bf16),
            pltpu.VMEM((COLS, PIECE, LANES), bf16),
            pltpu.VMEM((COLS, PIECE, LANES), bf16),
            pltpu.VMEM((2, PAIRS, BLK, LANES), bf16),
            pltpu.VMEM((ROWS, PAIRS, BLK, LANES), bf16),
            pltpu.VMEM((2, ROWS, 2, LANES // 2, LANES), bf16),
            pltpu.VMEM((2, 2 * ROWS, LANES // 2, LANES), bf16),
            dma((8,)),
            dma,
            dma((COLS,)),
            dma((COLS,)),
            dma((COLS,)),
            dma((COLS,)),
            dma((PAIRS, 11)),
            dma((2, PAIRS, 11)),
            dma((2, PAIRS)),
            dma((2, PAIRS)),
            dma((PAIRS, 7)),
            dma((PAIRS, 7)),
            dma((2, 2 * ROWS)),
            dma((2, 2 * ROWS)),
        ],
        compiler_params=pltpu.CompilerParams(
            collective_id=0, has_side_effects=True, vmem_limit_bytes=56 * 2**20
        ),
        cost_estimate=pl.CostEstimate(flops=7_000_000_000, bytes_accessed=30_000_000, transcendentals=0),
    )(block_cols, subspace, rotation, block_tiles)
    return pl.pallas_call(
        copy_out,
        out_shape=tuple(jax.ShapeDtypeStruct(x.shape, x.dtype) for x in results),
        in_specs=[vmem] * 3,
        out_specs=(vmem,) * 3,
    )(*results)


def solution(mesh):
    return jax.shard_map(
        local,
        mesh=mesh,
        in_specs=(P("col", "row"), P(), P("row", None, None, None), P("row", None)),
        out_specs=(P("col", "row"), P("col", "row"), P("col", "row")),
        check_vma=False,
    )
```

```python
import functools

import jax
import jax.numpy as jnp
from jax import lax
from jax.experimental import pallas as pl
from jax.experimental.pallas import tpu as pltpu
from jax.sharding import PartitionSpec as P

MESH = pl.DeviceIdType.MESH
DEGREE = 4
CENTER = 1.6
WIDTH = 0.9
ROWS = 8
COLS = 16
BLK = 192
SLOTS = 31
PAIRS = 4
HALF = PAIRS * BLK
PIECE = HALF // COLS
GROUP = 2
THREE_LEGS = 2
LANES = 128


def swap_halves(values):
    return pltpu.roll(values, LANES // 2, 1)


def kernel(
    cols, sub, rot_hbm, tiles_hbm, filt, gram, ray,
    field0, field1, tiles, rot, packed, raw, mixed, peer, every, sums, terms, parts,
    load_sem, rot_sem, out1, in1, out2, in2, row_out, row_in,
    sib_out, sib_in, col_out, col_in, sum_out, sum_in,
):
    r = lax.axis_index("row")
    c = lax.axis_index("col")
    core = lax.rem(c, 2)
    chip = c // 2
    sibling = c + 1 - 2 * core
    f32, bf16 = jnp.float32, jnp.bfloat16
    fields = (field0, field1)
    lane = lax.broadcasted_iota(jnp.int32, (1, LANES), 1) // (LANES // 2)

    loads = [pltpu.make_async_copy(tiles_hbm.at[i], tiles.at[i], load_sem.at[i]) for i in range(8)]
    rot_load = pltpu.make_async_copy(rot_hbm, rot, rot_sem)
    rot_load.start()
    for load in loads:
        load.start()

    def send(src, dst, out_sem, in_sem, to_row, to_col):
        copy = pltpu.make_async_remote_copy(
            src_ref=src, dst_ref=dst, send_sem=out_sem, recv_sem=in_sem,
            device_id=(to_row, to_col), device_id_type=MESH,
        )
        return copy

    far_steps = [
        (dy, dx, dk) for dy, dx in ((1, 2), (1, 1), (1, 3), (1, 0), (0, 2), (0, 1), (0, 3), (0, 0))
        for dk in (0, 1)
    ]
    far_steps.remove((0, 0, 0))

    def col_peer(d):
        dy, dx, dk = far_steps[d - 1]
        return 8 * lax.rem(c // 8 + dy, 2) + 2 * lax.rem(chip + dx, 4) + lax.rem(core + dk, 2)

    barrier = pltpu.get_barrier_semaphore()
    for d in range(1, COLS):
        pl.semaphore_signal(barrier, inc=1, device_id=(r, lax.rem(c + d, COLS)), device_id_type=MESH)
    for d in range(1, ROWS):
        for k in (0, 1):
            pl.semaphore_signal(
                barrier, inc=1, device_id=(lax.rem(r + d, ROWS), 2 * chip + k), device_id_type=MESH
            )

    natural = jnp.concatenate([sub[:, :HALF], sub[:, HALF:]], axis=0).astype(f32)
    packed[...] = natural.T.astype(bf16)
    for q in range(PAIRS):
        field1[PAIRS * r + q] = jnp.zeros((BLK, LANES), bf16)
    pl.semaphore_wait(barrier, COLS - 1 + 2 * (ROWS - 1))

    sends = []
    for d in range(1, COLS):
        to = col_peer(d)
        copy = send(
            packed.at[pl.ds(pl.multiple_of(to * PIECE, PIECE), PIECE)], raw.at[c],
            out1.at[d], in1.at[c], r, to,
        )
        copy.start()
        sends.append(copy)
    raw[c] = packed[pl.ds(pl.multiple_of(c * PIECE, PIECE), PIECE), :]
    for d in range(1, COLS):
        src = col_peer(COLS - d)
        send(packed.at[pl.ds(0, PIECE)], raw.at[src], out1.at[d], in1.at[src], r, src).wait_recv()
    rot_load.wait()
    left, right = [], []
    for e in range(COLS // 2):
        a, b = raw[2 * e].astype(f32), raw[2 * e + 1].astype(f32)
        left.append(jnp.where(lane == 0, a, swap_halves(b)))
        right.append(jnp.where(lane == 0, swap_halves(a), b))
    wide = jnp.concatenate(
        [jnp.concatenate(left, axis=1), jnp.concatenate(right, axis=1)], axis=0
    ).astype(bf16)
    rotated = jnp.dot(wide, rot[...], preferred_element_type=f32)
    for e in range(COLS // 2):
        a = rotated[:PIECE, e * LANES : (e + 1) * LANES]
        b = rotated[PIECE:, e * LANES : (e + 1) * LANES]
        mixed[2 * e] = jnp.where(lane == 0, a, swap_halves(b)).astype(bf16)
        mixed[2 * e + 1] = jnp.where(lane == 0, swap_halves(a), b).astype(bf16)

    def piece(of):
        return PAIRS * r + of // PAIRS, pl.ds(pl.multiple_of(lax.rem(of, PAIRS) * PIECE, PIECE), PIECE)

    for d in range(1, COLS):
        to = col_peer(d)
        copy = send(mixed.at[to], field0.at[*piece(c)], out2.at[d], in2.at[c], r, to)
        copy.start()
        sends.append(copy)
    field0[*piece(c)] = mixed[c]
    for d in range(1, COLS):
        src = col_peer(COLS - d)
        send(mixed.at[0], field0.at[*piece(src)], out2.at[d], in2.at[src], r, src).wait_recv()
    for copy in sends:
        copy.wait_send()

    def chunk_rows(q):
        return pl.ds(pl.multiple_of(q * BLK, BLK), BLK)

    z, y = r // 2, lax.rem(r, 2)

    def at(dz, dy):
        return 2 * lax.rem(z + dz + 4, 4) + (lax.rem(y + dy, 2))

    whole_pair, low, high = (0, BLK), (0, BLK // 2), (BLK // 2, BLK // 2)
    FIRST = (
        ((0, 0), (1, 0), whole_pair),
        ((0, 0), (-1, 0), whole_pair),
        ((0, 0), (0, 1), whole_pair),
    )

    def onward_plan(q):
        split = 160 if q < THREE_LEGS else 128
        by_z, by_y = (0, split), (split, BLK - split)
        plan = (
            (0, (-1, 0), (1, 0), low),
            (1, (1, 0), (-1, 0), high),
            (0, (-1, 0), (0, 1), by_y),
            (1, (1, 0), (0, 1), by_y),
            (2, (0, 1), (1, 0), by_z),
            (2, (0, 1), (-1, 0), by_z),
        )
        far = ((0, (-1, 0), (1, 1), low), (1, (1, 0), (-1, 1), high))
        return plan, far

    THIRD = (((2, 0), (0, 1), low), ((2, 0), (0, 1), high))

    def row_copy(par, q, n, src, to, part):
        view = fields[par].at[PAIRS * at(*src) + q, pl.ds(part[0], part[1])]
        return send(view, view, row_out.at[q, n], row_in.at[par, q, n], at(*to), c)

    def arrival(par, q, n, src, to, part):
        return row_copy(par, q, n, (src[0] - to[0], src[1] + to[1]), to, part)

    def spread(par, q):
        for n, (src, to, part) in enumerate(FIRST):
            row_copy(par, q, n, src, to, part).start()

    def onward(par, q):
        plan, far = onward_plan(q)
        steps = plan if q < THREE_LEGS else plan + far
        for n, (src, to, part) in enumerate(FIRST):
            arrival(par, q, n, src, to, part).wait_recv()
            for m, (after, src2, to2, part2) in enumerate(steps):
                if after == n:
                    row_copy(par, q, 3 + m, src2, to2, part2).start()

    def third(par, q):
        plan, _ = onward_plan(q)
        for m in range(2):
            arrival(par, q, 3 + m, *plan[m][1:]).wait_recv()
            row_copy(par, q, 9 + m, *THIRD[m]).start()

    def await_all(par):
        for q in range(PAIRS):
            plan, far = onward_plan(q)
            if q < THREE_LEGS:
                last = tuple((0, *step) for step in THIRD)
                pending = plan[2:] + last
            else:
                last = far
                pending = plan + last
            for n, (src, to, part) in enumerate(FIRST):
                row_copy(par, q, n, src, to, part).wait_send()
            for m, (_, src, to, part) in enumerate(plan + last):
                if (_, src, to, part) in pending:
                    arrival(par, q, 3 + m, src, to, part).wait_recv()
                row_copy(par, q, 3 + m, src, to, part).wait_send()

    def picked(par, i, s):
        col = cols[i, s]
        part = fields[par][((col >> 3) << 2) + (col & 3)]
        return jnp.where(lane == ((col >> 2) & 1), part, jnp.zeros_like(part))

    def applied(par, q):
        totals = [jnp.zeros((BLK, LANES), f32)] * 2
        for s in range(0, SLOTS, GROUP):
            slots = range(s, min(s + GROUP, SLOTS))
            for n in range(2):
                i = q + PAIRS * n
                wide_tiles = jnp.concatenate([tiles[i, t] for t in slots], axis=1)
                blocks = jnp.concatenate([picked(par, i, t) for t in slots], axis=0)
                totals[n] += jnp.dot(wide_tiles, blocks, preferred_element_type=f32)
        first, second = totals
        return jnp.where(lane == 0, first + swap_halves(first), second + swap_halves(second))

    def next_level(par, q, scale):
        now = fields[par][PAIRS * r + q].astype(f32)
        before = fields[1 - par][PAIRS * r + q].astype(f32)
        level = scale * (applied(par, q) - CENTER * now) - before
        fields[1 - par][PAIRS * r + q] = level.astype(bf16)

    for q in range(PAIRS):
        spread(0, q)
    for q in range(PAIRS):
        onward(0, q)
    for q in range(THREE_LEGS):
        third(0, q)
    for load in loads:
        load.wait()

    def sib_copy(which, q):
        src = fields[which].at[PAIRS * r + q]
        return send(
            src, peer.at[which, q], sib_out.at[which, q], sib_in.at[which, q], r, sibling
        )

    def merged_pair(which, q):
        own = fields[which][PAIRS * r + q].astype(f32)
        other = swap_halves(peer[which, q].astype(f32))
        return jnp.where(lane == core, own, other)

    high_y, x = chip // 4, lax.rem(chip, 4)
    ACROSS = ((1, 0), (3, 0), (2, 0))
    COL = ((0, 1), *ACROSS)

    def chip_at(dx, dy):
        return 4 * lax.rem(high_y + dy, 2) + lax.rem(x + dx, 4)

    def col_copy(q, n, source_chip, to):
        view = every.at[source_chip, q]
        return send(view, view, col_out.at[q, n], col_in.at[q, n], r, 2 * to + core)

    def col_first(q):
        sib_copy(0, q).wait()
        every[chip, q] = merged_pair(0, q).astype(bf16)
        for n, to in enumerate(COL):
            col_copy(q, n, chip, chip_at(*to)).start()

    def col_onward(q):
        other = chip_at(0, 1)
        col_copy(q, 0, other, other).wait_recv()
        for n, to in enumerate(ACROSS):
            col_copy(q, 4 + n, other, chip_at(*to)).start()

    def col_await():
        def step(q, carry):
            other = chip_at(0, 1)
            col_copy(q, 0, chip, other).wait_send()
            for n, to in enumerate(ACROSS):
                col_copy(q, 1 + n, chip, chip_at(*to)).wait_send()
                col_copy(q, 4 + n, other, chip_at(*to)).wait_send()
                col_copy(q, 1 + n, chip_at(4 - to[0], 0), chip_at(*to)).wait_recv()
                col_copy(q, 4 + n, chip_at(4 - to[0], 1), chip_at(*to)).wait_recv()
            return carry

        lax.fori_loop(0, PAIRS, step, 0)

    def one_level(par, scale, last):
        await_all(par)

        def pair(q, carry):
            next_level(par, q, scale)
            spread(1 - par, q)
            if last is not None:

                @pl.when(last)
                def _():
                    sib_copy(0, q).start()

                    @pl.when(q >= 1)
                    def _():
                        col_first(q - 1)

            return carry

        lax.fori_loop(0, PAIRS, pair, 0)
        if last is not None:

            @pl.when(last)
            def _():
                col_first(PAIRS - 1)

        for q in range(PAIRS):
            onward(1 - par, q)
        for q in range(THREE_LEGS):
            third(1 - par, q)

    def two_levels(k, carry):
        one_level(0, jnp.where(k == 0, 1.0 / WIDTH, 2.0 / WIDTH), None)
        one_level(1, 2.0 / WIDTH, k == DEGREE // 2 - 1)
        return carry

    lax.fori_loop(0, DEGREE // 2, two_levels, 0)

    lax.fori_loop(0, PAIRS, lambda q, carry: (col_onward(q), carry)[1], 0)
    flat = jnp.concatenate([field0[PAIRS * r + q] for q in range(PAIRS)], axis=0)
    flat = flat.astype(f32).T.astype(bf16)
    filt[:, :HALF] = flat[: LANES // 2]
    filt[:, HALF:] = flat[LANES // 2 :]
    own_half = every[chip].reshape(HALF, LANES).astype(f32).T.astype(bf16)
    await_all(0)

    source = 2 * r + core

    def sum_copy(w, n, to_row, to_core, src):
        return send(
            terms.at[w, to_row, to_core], parts.at[w, src], sum_out.at[w, n], sum_in.at[w, src],
            to_row, 2 * chip + to_core,
        )

    row_steps = [
        (dz, dy, dk) for dz, dy in ((2, 1), (1, 1), (-1, 1), (2, 0), (1, 0), (-1, 0), (0, 1), (0, 0))
        for dk in (0, 1)
    ]
    row_steps.remove((0, 0, 0))

    def member(n):
        dz, dy, dk = row_steps[n - 1]
        to_row, to_core = at(dz, dy), lax.rem(core + dk, 2)
        return to_row, to_core, 2 * to_row + to_core

    def send_terms(w, product_with):
        for e in range(ROWS):
            product = product_with(e).astype(bf16)
            terms[w, e, 0] = product[: LANES // 2]
            terms[w, e, 1] = product[LANES // 2 :]
        for n in range(1, 2 * ROWS):
            to_row, to_core, _ = member(n)
            sum_copy(w, n, to_row, to_core, source).start()
        parts[w, source] = terms[w, r, core]

    def add_terms(w):
        for n in range(1, 2 * ROWS):
            to_row, to_core, index = member(n)
            sum_copy(w, n, r, core, index).wait_recv()
            sum_copy(w, n, to_row, to_core, source).wait_send()
        total = parts[w, 0].astype(f32)
        for n in range(1, 2 * ROWS):
            total += parts[w, n].astype(f32)
        return total * (1.0 / (ROWS * 2 * HALF))

    def image_pair(q):
        field1[PAIRS * r + q] = applied(0, q).astype(bf16)
        sib_copy(1, q).start()

    def image_step(q, carry):
        image_pair(q)

        @pl.when(q == PAIRS - 2)
        def _():
            col_await()
            send_terms(
                0,
                lambda e: jnp.dot(
                    own_half, every[e].reshape(HALF, LANES), preferred_element_type=f32
                ),
            )

        return carry

    lax.fori_loop(0, PAIRS, image_step, 0)
    halves = []
    for q in range(PAIRS - 1):
        sib_copy(1, q).wait()
        halves.append(merged_pair(1, q))
    early = jnp.concatenate(halves, axis=0).T.astype(bf16)
    for e in range(ROWS):
        blocks = every[e, : PAIRS - 1].reshape(HALF - BLK, LANES)
        sums[e] = jnp.dot(early, blocks, preferred_element_type=f32)
    sib_copy(1, PAIRS - 1).wait()
    late = merged_pair(1, PAIRS - 1).T.astype(bf16)
    send_terms(
        1, lambda e: sums[e] + jnp.dot(late, every[e, PAIRS - 1], preferred_element_type=f32)
    )
    gram[...] = add_terms(0)
    ray[...] = add_terms(1)


def copy_out(filt, gram, ray, filt_out, gram_out, ray_out):
    filt_out[...] = filt[...]
    gram_out[...] = gram[...]
    ray_out[...] = ray[...]


def local(subspace, rotation, block_tiles, block_cols):
    bf16, f32 = jnp.bfloat16, jnp.float32
    vmem = pl.BlockSpec(memory_space=pltpu.VMEM)
    dma = pltpu.SemaphoreType.DMA
    results = pl.pallas_call(
        kernel,
        out_shape=(
            jax.ShapeDtypeStruct(subspace.shape, bf16),
            jax.ShapeDtypeStruct((LANES // 2, LANES), f32),
            jax.ShapeDtypeStruct((LANES // 2, LANES), f32),
        ),
        in_specs=[
            pl.BlockSpec(memory_space=pltpu.SMEM),
            vmem,
            pl.BlockSpec(memory_space=pl.ANY),
            pl.BlockSpec(memory_space=pl.ANY),
        ],
        out_specs=(vmem, vmem, vmem),
        scratch_shapes=[
            pltpu.VMEM((ROWS * PAIRS, BLK, LANES), bf16),
            pltpu.VMEM((ROWS * PAIRS, BLK, LANES), bf16),
            pltpu.VMEM(block_tiles.shape, bf16),
            pltpu.VMEM(rotation.shape, bf16),
            pltpu.VMEM((HALF, LANES), bf16),
            pltpu.VMEM((COLS, PIECE, LANES), bf16),
            pltpu.VMEM((COLS, PIECE, LANES), bf16),
            pltpu.VMEM((2, PAIRS, BLK, LANES), bf16),
            pltpu.VMEM((ROWS, PAIRS, BLK, LANES), bf16),
            pltpu.VMEM((ROWS, LANES, LANES), f32),
            pltpu.VMEM((2, ROWS, 2, LANES // 2, LANES), bf16),
            pltpu.VMEM((2, 2 * ROWS, LANES // 2, LANES), bf16),
            dma((8,)),
            dma,
            dma((COLS,)),
            dma((COLS,)),
            dma((COLS,)),
            dma((COLS,)),
            dma((PAIRS, 11)),
            dma((2, PAIRS, 11)),
            dma((2, PAIRS)),
            dma((2, PAIRS)),
            dma((PAIRS, 7)),
            dma((PAIRS, 7)),
            dma((2, 2 * ROWS)),
            dma((2, 2 * ROWS)),
        ],
        compiler_params=pltpu.CompilerParams(
            collective_id=0, has_side_effects=True, vmem_limit_bytes=56 * 2**20
        ),
        cost_estimate=pl.CostEstimate(flops=7_000_000_000, bytes_accessed=30_000_000, transcendentals=0),
    )(block_cols, subspace, rotation, block_tiles)
    return pl.pallas_call(
        copy_out,
        out_shape=tuple(jax.ShapeDtypeStruct(x.shape, x.dtype) for x in results),
        in_specs=[vmem] * 3,
        out_specs=(vmem,) * 3,
    )(*results)


def solution(mesh):
    return jax.shard_map(
        local,
        mesh=mesh,
        in_specs=(P("col", "row"), P(), P("row", None, None, None), P("row", None)),
        out_specs=(P("col", "row"), P("col", "row"), P("col", "row")),
        check_vma=False,
    )
```

```python
import functools

import jax
import jax.numpy as jnp
from jax import lax
from jax.experimental import pallas as pl
from jax.experimental.pallas import tpu as pltpu
from jax.sharding import PartitionSpec as P

MESH = pl.DeviceIdType.MESH
DEGREE = 4
CENTER = 1.6
WIDTH = 0.9
ROWS = 8
COLS = 16
BLK = 192
SLOTS = 31
PAIRS = 4
HALF = PAIRS * BLK
PIECE = HALF // COLS
GROUP = 2
THREE_LEGS = 2
LANES = 128


def swap_halves(values):
    return pltpu.roll(values, LANES // 2, 1)


def kernel(
    cols, sub, rot_hbm, tiles_hbm, filt, gram, ray,
    field0, field1, tiles, rot, packed, raw, mixed, peer, every, sums, terms, parts,
    load_sem, rot_sem, out1, in1, out2, in2, row_out, row_in,
    sib_out, sib_in, col_out, col_in, sum_out, sum_in,
):
    r = lax.axis_index("row")
    c = lax.axis_index("col")
    core = lax.rem(c, 2)
    chip = c // 2
    sibling = c + 1 - 2 * core
    f32, bf16 = jnp.float32, jnp.bfloat16
    fields = (field0, field1)
    lane = lax.broadcasted_iota(jnp.int32, (1, LANES), 1) // (LANES // 2)

    loads = [pltpu.make_async_copy(tiles_hbm.at[i], tiles.at[i], load_sem.at[i]) for i in range(8)]
    rot_load = pltpu.make_async_copy(rot_hbm, rot, rot_sem)

    def send(src, dst, out_sem, in_sem, to_row, to_col):
        copy = pltpu.make_async_remote_copy(
            src_ref=src, dst_ref=dst, send_sem=out_sem, recv_sem=in_sem,
            device_id=(to_row, to_col), device_id_type=MESH,
        )
        return copy

    far_steps = [
        (dy, dx, dk) for dy, dx in ((1, 2), (1, 1), (1, 3), (1, 0), (0, 2), (0, 1), (0, 3), (0, 0))
        for dk in (0, 1)
    ]
    far_steps.remove((0, 0, 0))

    def col_peer(d):
        dy, dx, dk = far_steps[d - 1]
        return 8 * lax.rem(c // 8 + dy, 2) + 2 * lax.rem(chip + dx, 4) + lax.rem(core + dk, 2)

    barrier = pltpu.get_barrier_semaphore()
    for d in range(1, COLS):
        pl.semaphore_signal(barrier, inc=1, device_id=(r, lax.rem(c + d, COLS)), device_id_type=MESH)
    for d in range(1, ROWS):
        for k in (0, 1):
            pl.semaphore_signal(
                barrier, inc=1, device_id=(lax.rem(r + d, ROWS), 2 * chip + k), device_id_type=MESH
            )

    rot_load.start()
    for load in loads:
        load.start()

    natural = jnp.concatenate([sub[:, :HALF], sub[:, HALF:]], axis=0).astype(f32)
    packed[...] = natural.T.astype(bf16)
    for q in range(PAIRS):
        field1[PAIRS * r + q] = jnp.zeros((BLK, LANES), bf16)
    pl.semaphore_wait(barrier, COLS - 1 + 2 * (ROWS - 1))

    sends = []
    for d in range(1, COLS):
        to = col_peer(d)
        copy = send(
            packed.at[pl.ds(pl.multiple_of(to * PIECE, PIECE), PIECE)], raw.at[c],
            out1.at[d], in1.at[c], r, to,
        )
        copy.start()
        sends.append(copy)
    raw[c] = packed[pl.ds(pl.multiple_of(c * PIECE, PIECE), PIECE), :]
    for d in range(1, COLS):
        src = col_peer(COLS - d)
        send(packed.at[pl.ds(0, PIECE)], raw.at[src], out1.at[d], in1.at[src], r, src).wait_recv()
    rot_load.wait()
    left, right = [], []
    for e in range(COLS // 2):
        a, b = raw[2 * e].astype(f32), raw[2 * e + 1].astype(f32)
        left.append(jnp.where(lane == 0, a, swap_halves(b)))
        right.append(jnp.where(lane == 0, swap_halves(a), b))
    wide = jnp.concatenate(
        [jnp.concatenate(left, axis=1), jnp.concatenate(right, axis=1)], axis=0
    ).astype(bf16)
    rotated = jnp.dot(wide, rot[...], preferred_element_type=f32)
    for e in range(COLS // 2):
        a = rotated[:PIECE, e * LANES : (e + 1) * LANES]
        b = rotated[PIECE:, e * LANES : (e + 1) * LANES]
        mixed[2 * e] = jnp.where(lane == 0, a, swap_halves(b)).astype(bf16)
        mixed[2 * e + 1] = jnp.where(lane == 0, swap_halves(a), b).astype(bf16)

    def piece(of):
        return PAIRS * r + of // PAIRS, pl.ds(pl.multiple_of(lax.rem(of, PAIRS) * PIECE, PIECE), PIECE)

    for d in range(1, COLS):
        to = col_peer(d)
        copy = send(mixed.at[to], field0.at[*piece(c)], out2.at[d], in2.at[c], r, to)
        copy.start()
        sends.append(copy)
    field0[*piece(c)] = mixed[c]
    for d in range(1, COLS):
        src = col_peer(COLS - d)
        send(mixed.at[0], field0.at[*piece(src)], out2.at[d], in2.at[src], r, src).wait_recv()
    for copy in sends:
        copy.wait_send()

    def chunk_rows(q):
        return pl.ds(pl.multiple_of(q * BLK, BLK), BLK)

    z, y = r // 2, lax.rem(r, 2)

    def at(dz, dy):
        return 2 * lax.rem(z + dz + 4, 4) + (lax.rem(y + dy, 2))

    whole_pair, low, high = (0, BLK), (0, BLK // 2), (BLK // 2, BLK // 2)
    FIRST = (
        ((0, 0), (1, 0), whole_pair),
        ((0, 0), (-1, 0), whole_pair),
        ((0, 0), (0, 1), whole_pair),
    )

    def onward_plan(q):
        split = 160 if q < THREE_LEGS else 128
        by_z, by_y = (0, split), (split, BLK - split)
        plan = (
            (0, (-1, 0), (1, 0), low),
            (1, (1, 0), (-1, 0), high),
            (0, (-1, 0), (0, 1), by_y),
            (1, (1, 0), (0, 1), by_y),
            (2, (0, 1), (1, 0), by_z),
            (2, (0, 1), (-1, 0), by_z),
        )
        far = ((0, (-1, 0), (1, 1), low), (1, (1, 0), (-1, 1), high))
        return plan, far

    THIRD = (((2, 0), (0, 1), low), ((2, 0), (0, 1), high))

    def row_copy(par, q, n, src, to, part):
        view = fields[par].at[PAIRS * at(*src) + q, pl.ds(part[0], part[1])]
        return send(view, view, row_out.at[q, n], row_in.at[par, q, n], at(*to), c)

    def arrival(par, q, n, src, to, part):
        return row_copy(par, q, n, (src[0] - to[0], src[1] + to[1]), to, part)

    def spread(par, q):
        for n, (src, to, part) in enumerate(FIRST):
            row_copy(par, q, n, src, to, part).start()

    def onward(par, q):
        plan, far = onward_plan(q)
        steps = plan if q < THREE_LEGS else plan + far
        for n, (src, to, part) in enumerate(FIRST):
            arrival(par, q, n, src, to, part).wait_recv()
            for m, (after, src2, to2, part2) in enumerate(steps):
                if after == n:
                    row_copy(par, q, 3 + m, src2, to2, part2).start()

    def third(par, q):
        plan, _ = onward_plan(q)
        for m in range(2):
            arrival(par, q, 3 + m, *plan[m][1:]).wait_recv()
            row_copy(par, q, 9 + m, *THIRD[m]).start()

    def await_all(par):
        for q in range(PAIRS):
            plan, far = onward_plan(q)
            if q < THREE_LEGS:
                last = tuple((0, *step) for step in THIRD)
                pending = plan[2:] + last
            else:
                last = far
                pending = plan + last
            for n, (src, to, part) in enumerate(FIRST):
                row_copy(par, q, n, src, to, part).wait_send()
            for m, (_, src, to, part) in enumerate(plan + last):
                if (_, src, to, part) in pending:
                    arrival(par, q, 3 + m, src, to, part).wait_recv()
                row_copy(par, q, 3 + m, src, to, part).wait_send()

    def picked(par, i, s):
        col = cols[i, s]
        part = fields[par][((col >> 3) << 2) + (col & 3)]
        return jnp.where(lane == ((col >> 2) & 1), part, jnp.zeros_like(part))

    def applied(par, q):
        totals = [jnp.zeros((BLK, LANES), f32)] * 2
        for s in range(0, SLOTS, GROUP):
            slots = range(s, min(s + GROUP, SLOTS))
            for n in range(2):
                i = q + PAIRS * n
                wide_tiles = jnp.concatenate([tiles[i, t] for t in slots], axis=1)
                blocks = jnp.concatenate([picked(par, i, t) for t in slots], axis=0)
                totals[n] += jnp.dot(wide_tiles, blocks, preferred_element_type=f32)
        first, second = totals
        return jnp.where(lane == 0, first + swap_halves(first), second + swap_halves(second))

    def next_level(par, q, scale):
        now = fields[par][PAIRS * r + q].astype(f32)
        before = fields[1 - par][PAIRS * r + q].astype(f32)
        level = scale * (applied(par, q) - CENTER * now) - before
        fields[1 - par][PAIRS * r + q] = level.astype(bf16)

    for q in range(PAIRS):
        spread(0, q)
    for q in range(PAIRS):
        onward(0, q)
    for q in range(THREE_LEGS):
        third(0, q)
    for load in loads:
        load.wait()

    def sib_copy(which, q):
        src = fields[which].at[PAIRS * r + q]
        return send(
            src, peer.at[which, q], sib_out.at[which, q], sib_in.at[which, q], r, sibling
        )

    def merged_pair(which, q):
        own = fields[which][PAIRS * r + q].astype(f32)
        other = swap_halves(peer[which, q].astype(f32))
        return jnp.where(lane == core, own, other)

    high_y, x = chip // 4, lax.rem(chip, 4)
    ACROSS = ((1, 0), (3, 0), (2, 0))
    COL = ((0, 1), *ACROSS)

    def chip_at(dx, dy):
        return 4 * lax.rem(high_y + dy, 2) + lax.rem(x + dx, 4)

    def col_copy(q, n, source_chip, to):
        view = every.at[source_chip, q]
        return send(view, view, col_out.at[q, n], col_in.at[q, n], r, 2 * to + core)

    def col_first(q):
        sib_copy(0, q).wait()
        every[chip, q] = merged_pair(0, q).astype(bf16)
        for n, to in enumerate(COL):
            col_copy(q, n, chip, chip_at(*to)).start()

    def col_onward(q):
        other = chip_at(0, 1)
        col_copy(q, 0, other, other).wait_recv()
        for n, to in enumerate(ACROSS):
            col_copy(q, 4 + n, other, chip_at(*to)).start()

    def col_await():
        def step(q, carry):
            other = chip_at(0, 1)
            col_copy(q, 0, chip, other).wait_send()
            for n, to in enumerate(ACROSS):
                col_copy(q, 1 + n, chip, chip_at(*to)).wait_send()
                col_copy(q, 4 + n, other, chip_at(*to)).wait_send()
                col_copy(q, 1 + n, chip_at(4 - to[0], 0), chip_at(*to)).wait_recv()
                col_copy(q, 4 + n, chip_at(4 - to[0], 1), chip_at(*to)).wait_recv()
            return carry

        lax.fori_loop(0, PAIRS, step, 0)

    def one_level(par, scale, last):
        await_all(par)

        def pair(q, carry):
            next_level(par, q, scale)
            spread(1 - par, q)
            if last is not None:

                @pl.when(last)
                def _():
                    sib_copy(0, q).start()

                    @pl.when(q >= 1)
                    def _():
                        col_first(q - 1)

            return carry

        lax.fori_loop(0, PAIRS, pair, 0)
        if last is not None:

            @pl.when(last)
            def _():
                col_first(PAIRS - 1)

        for q in range(PAIRS):
            onward(1 - par, q)
        for q in range(THREE_LEGS):
            third(1 - par, q)

    def two_levels(k, carry):
        one_level(0, jnp.where(k == 0, 1.0 / WIDTH, 2.0 / WIDTH), None)
        one_level(1, 2.0 / WIDTH, k == DEGREE // 2 - 1)
        return carry

    lax.fori_loop(0, DEGREE // 2, two_levels, 0)

    lax.fori_loop(0, PAIRS, lambda q, carry: (col_onward(q), carry)[1], 0)
    flat = jnp.concatenate([field0[PAIRS * r + q] for q in range(PAIRS)], axis=0)
    flat = flat.astype(f32).T.astype(bf16)
    filt[:, :HALF] = flat[: LANES // 2]
    filt[:, HALF:] = flat[LANES // 2 :]
    own_half = every[chip].reshape(HALF, LANES).astype(f32).T.astype(bf16)
    await_all(0)

    source = 2 * r + core

    def sum_copy(w, n, to_row, to_core, src):
        return send(
            terms.at[w, to_row, to_core], parts.at[w, src], sum_out.at[w, n], sum_in.at[w, src],
            to_row, 2 * chip + to_core,
        )

    row_steps = [
        (dz, dy, dk) for dz, dy in ((2, 1), (1, 1), (-1, 1), (2, 0), (1, 0), (-1, 0), (0, 1), (0, 0))
        for dk in (0, 1)
    ]
    row_steps.remove((0, 0, 0))

    def member(n):
        dz, dy, dk = row_steps[n - 1]
        to_row, to_core = at(dz, dy), lax.rem(core + dk, 2)
        return to_row, to_core, 2 * to_row + to_core

    def send_terms(w, product_with):
        for e in range(ROWS):
            product = product_with(e).astype(bf16)
            terms[w, e, 0] = product[: LANES // 2]
            terms[w, e, 1] = product[LANES // 2 :]
        for n in range(1, 2 * ROWS):
            to_row, to_core, _ = member(n)
            sum_copy(w, n, to_row, to_core, source).start()
        parts[w, source] = terms[w, r, core]

    def add_terms(w):
        for n in range(1, 2 * ROWS):
            to_row, to_core, index = member(n)
            sum_copy(w, n, r, core, index).wait_recv()
            sum_copy(w, n, to_row, to_core, source).wait_send()
        total = parts[w, 0].astype(f32)
        for n in range(1, 2 * ROWS):
            total += parts[w, n].astype(f32)
        return total * (1.0 / (ROWS * 2 * HALF))

    def image_pair(q):
        field1[PAIRS * r + q] = applied(0, q).astype(bf16)
        sib_copy(1, q).start()

    def image_step(q, carry):
        image_pair(q)

        @pl.when(q == PAIRS - 2)
        def _():
            col_await()
            send_terms(
                0,
                lambda e: jnp.dot(
                    own_half, every[e].reshape(HALF, LANES), preferred_element_type=f32
                ),
            )

        return carry

    lax.fori_loop(0, PAIRS, image_step, 0)
    halves = []
    for q in range(PAIRS - 1):
        sib_copy(1, q).wait()
        halves.append(merged_pair(1, q))
    early = jnp.concatenate(halves, axis=0).T.astype(bf16)
    for e in range(ROWS):
        blocks = every[e, : PAIRS - 1].reshape(HALF - BLK, LANES)
        sums[e] = jnp.dot(early, blocks, preferred_element_type=f32)
    sib_copy(1, PAIRS - 1).wait()
    late = merged_pair(1, PAIRS - 1).T.astype(bf16)
    send_terms(
        1, lambda e: sums[e] + jnp.dot(late, every[e, PAIRS - 1], preferred_element_type=f32)
    )
    gram[...] = add_terms(0)
    ray[...] = add_terms(1)


def copy_out(filt, gram, ray, filt_out, gram_out, ray_out):
    filt_out[...] = filt[...]
    gram_out[...] = gram[...]
    ray_out[...] = ray[...]


def local(subspace, rotation, block_tiles, block_cols):
    bf16, f32 = jnp.bfloat16, jnp.float32
    vmem = pl.BlockSpec(memory_space=pltpu.VMEM)
    dma = pltpu.SemaphoreType.DMA
    results = pl.pallas_call(
        kernel,
        out_shape=(
            jax.ShapeDtypeStruct(subspace.shape, bf16),
            jax.ShapeDtypeStruct((LANES // 2, LANES), f32),
            jax.ShapeDtypeStruct((LANES // 2, LANES), f32),
        ),
        in_specs=[
            pl.BlockSpec(memory_space=pltpu.SMEM),
            vmem,
            pl.BlockSpec(memory_space=pl.ANY),
            pl.BlockSpec(memory_space=pl.ANY),
        ],
        out_specs=(vmem, vmem, vmem),
        scratch_shapes=[
            pltpu.VMEM((ROWS * PAIRS, BLK, LANES), bf16),
            pltpu.VMEM((ROWS * PAIRS, BLK, LANES), bf16),
            pltpu.VMEM(block_tiles.shape, bf16),
            pltpu.VMEM(rotation.shape, bf16),
            pltpu.VMEM((HALF, LANES), bf16),
            pltpu.VMEM((COLS, PIECE, LANES), bf16),
            pltpu.VMEM((COLS, PIECE, LANES), bf16),
            pltpu.VMEM((2, PAIRS, BLK, LANES), bf16),
            pltpu.VMEM((ROWS, PAIRS, BLK, LANES), bf16),
            pltpu.VMEM((ROWS, LANES, LANES), f32),
            pltpu.VMEM((2, ROWS, 2, LANES // 2, LANES), bf16),
            pltpu.VMEM((2, 2 * ROWS, LANES // 2, LANES), bf16),
            dma((8,)),
            dma,
            dma((COLS,)),
            dma((COLS,)),
            dma((COLS,)),
            dma((COLS,)),
            dma((PAIRS, 11)),
            dma((2, PAIRS, 11)),
            dma((2, PAIRS)),
            dma((2, PAIRS)),
            dma((PAIRS, 7)),
            dma((PAIRS, 7)),
            dma((2, 2 * ROWS)),
            dma((2, 2 * ROWS)),
        ],
        compiler_params=pltpu.CompilerParams(
            collective_id=0, has_side_effects=True, vmem_limit_bytes=56 * 2**20
        ),
        cost_estimate=pl.CostEstimate(flops=7_000_000_000, bytes_accessed=30_000_000, transcendentals=0),
    )(block_cols, subspace, rotation, block_tiles)
    return pl.pallas_call(
        copy_out,
        out_shape=tuple(jax.ShapeDtypeStruct(x.shape, x.dtype) for x in results),
        in_specs=[vmem] * 3,
        out_specs=(vmem,) * 3,
    )(*results)


def solution(mesh):
    return jax.shard_map(
        local,
        mesh=mesh,
        in_specs=(P("col", "row"), P(), P("row", None, None, None), P("row", None)),
        out_specs=(P("col", "row"), P("col", "row"), P("col", "row")),
        check_vma=False,
    )
```
